32 devices in a mesh: dp: 4 (over x, core), expert: 4 (over z), fsdp: 2 (over y).
Axes of the slice: x: 2, y: 2, z: 4, core: 2. Of those that a mesh axis runs over, the one named last changes fastest.
Arguments:
- grads: float32 [4, 16, 256, 512], P('dp', 'expert', 'fsdp'), may hold values from -65 to 65
- owner_slot: int32 [16], P('expert'), may hold values from 0 to 7, as said below
- momentum: bfloat16 [32, 256, 512], P(('dp', 'expert', 'fsdp')), may hold values from -6 to 6
Outputs:
- updates: bfloat16 [16, 256, 512], P('expert', 'fsdp')
- new_momentum: bfloat16 [32, 256, 512], P(('dp', 'expert', 'fsdp'))
The draws below stay inside these ranges and needn't reach their ends.
Inputs may be any that keep to these rules, and one draw needn't show every extreme that they name: Within each group e, the 4 entries owner_slot[e * 4 + j] are distinct; in every group some owner o holds all 1 of its slots.
All inputs are finite; a program needn't handle non-finite values.
Results may differ from the reference program's by a relative error of at most 0.001.
Values may be sent and summed in bfloat16 or wider, within the bound.
No kernel may reach another device: no remote copies, remote signals or barrier semaphores. Data moves between devices by JAX's collectives and lax.ppermute only.
A program may use at most 64 MiB of HBM per device.

```python
import math
import jax
import jax.numpy as jnp
from jax import lax

R = 256
C = 512
ITERS = 5
CAP = 1
REPLICAS = 4
GROUPS = 4
SHARDS = 2
SLOTS = 8
MAT_E = 4
M = 16
SLOTS_ALL = 32


def draw_grads(key, part):
    key = jax.random.fold_in(key, 7)
    k_rows, k_cols, k_base = jax.random.split(key, 3)
    spread = math.log(10.0)
    row_scale = jnp.exp(jax.random.uniform(k_rows, (1, M, R, 1), jnp.float32) * spread)
    col_scale = jnp.exp(jax.random.uniform(k_cols, (1, M, 1, C), jnp.float32) * spread)
    base = jnp.clip(jax.random.normal(k_base, (REPLICAS, M, R, C), jnp.float32), -6.0, 6.0)
    return base * row_scale * col_scale * 0.03


def draw_owner_slot(key, part):
    key = jax.random.fold_in(key, 5)

    def one_group(group_key):
        k_order, k_shuffle = jax.random.split(group_key)
        order = jax.random.permutation(k_order, SLOTS).astype(jnp.int32)
        fullest = order[0] // CAP
        positions = jnp.arange(SLOTS, dtype=jnp.int32)
        ranking = jnp.zeros((SLOTS,), jnp.int32).at[order].set(positions)
        priority = jnp.where(positions // CAP == fullest, positions - SLOTS, ranking)
        chosen = jnp.argsort(priority, stable=True)[:MAT_E].astype(jnp.int32)
        shuffle = jax.random.permutation(k_shuffle, MAT_E)
        return chosen[shuffle].astype(jnp.int32)
    group_keys = jax.random.split(key, M // MAT_E)
    return jax.vmap(one_group)(group_keys).reshape(M).astype(jnp.int32)


def level_of(key, dims, shards, least, largest):
    gain = 1.0
    for position, blocks in shards:
        draws = jax.random.uniform(jax.random.fold_in(jax.random.fold_in(key, 6), position), (blocks,), jnp.float32, least / len(shards), largest / len(shards))
        gain = gain * jnp.repeat(jnp.exp(draws), dims[position] // blocks).reshape((-1,) + (1,) * (len(dims) - 1 - position))
    return gain


def normal_values(key, dims, width, reach, cuts=(), kind=jnp.bfloat16):
    gain = level_of(key, dims, cuts, -0.22, 0.18) if cuts else 1.0
    array = jax.random.normal(key, dims, jnp.float32) * width * gain
    return jnp.minimum(jnp.maximum(array, -reach), reach).astype(kind)


def setup_inputs(seed: int = 0) -> dict:
    keys = jax.random.split(jax.random.key(seed), 4)
    return {
        "grads": draw_grads(jax.random.fold_in(keys[3], 71), 0),
        "owner_slot": draw_owner_slot(jax.random.fold_in(keys[3], 71), 0),
        "momentum": normal_values(keys[2], (SLOTS_ALL, R, C), 1.0, 6.0, ((0, 32),)),
    }


COEF_A = 3.4445
COEF_B = -4.775
COEF_C = 2.0315
MOMENT = 0.95

def orthogonalize(stack):
    norms = jnp.sqrt(lax.optimization_barrier(jnp.sum(stack * stack, axis=(1, 2), keepdims=True)))
    current = stack / (norms + 1e-07)
    for step in range(ITERS):
        gram = jnp.einsum('krc,ksc->krs', current, current, precision=lax.Precision.HIGHEST)
        square = jnp.einsum('krs,kst->krt', gram, gram, precision=lax.Precision.HIGHEST)
        poly = COEF_B * gram + COEF_C * square
        current = COEF_A * current + jnp.einsum('krs,ksc->krc', poly, current, precision=lax.Precision.HIGHEST)
    return current

def reference(grads, owner_slot, momentum):
    total = lax.optimization_barrier(jnp.sum(grads, axis=0))
    matrix_ids = jnp.arange(M, dtype=jnp.int32)
    group_of = matrix_ids // MAT_E
    owner = owner_slot // CAP
    within = owner_slot % CAP
    replica_of = owner // SHARDS
    shard_of = owner % SHARDS
    home = (((replica_of * GROUPS + group_of) * SHARDS + shard_of) * CAP + within).astype(jnp.int32)
    buffer = MOMENT * momentum.astype(jnp.float32)
    buffer = buffer.at[home].add(total)
    new_momentum = buffer.astype(jnp.bfloat16)
    nesterov = total + MOMENT * buffer[home]
    factor = 0.2 * math.sqrt(max(R, C))
    ortho = lax.map(lambda single: orthogonalize(single[None])[0], nesterov)
    updates = (factor * ortho).astype(jnp.bfloat16)
    return (updates, new_momentum)
```

```python
import functools
import math

import jax
import jax.numpy as jnp
from jax import lax
from jax.experimental import pallas as pl
from jax.experimental.pallas import tpu as pltpu
from jax.sharding import PartitionSpec as P

R = 256
C = 512
ITERS = 5


COEF_A = 3.4445
COEF_B = -4.775
COEF_C = 2.0315
MOMENT = 0.95
FACTOR = 0.2 * math.sqrt(max(R, C))

AXES = ("dp", "fsdp")
SMEM = pl.BlockSpec(memory_space=pltpu.SMEM)
VMEM = pl.BlockSpec(memory_space=pltpu.VMEM)
ANY = pl.BlockSpec(memory_space=pl.ANY)


def orthogonalize(stack):
    norms = jnp.sqrt(jnp.sum(stack * stack, axis=(1, 2), keepdims=True))
    current = stack / (norms + 1e-07)
    for step in range(ITERS):
        gram = jnp.einsum("krc,ksc->krs", current, current, precision=lax.Precision.HIGHEST)
        square = jnp.einsum("krs,kst->krt", gram, gram, precision=lax.Precision.HIGHEST)
        poly = COEF_B * gram + COEF_C * square
        current = COEF_A * current + jnp.einsum(
            "krs,ksc->krc", poly, current, precision=lax.Precision.HIGHEST
        )
    return current


def per_device_general(grads, owner_slot, momentum):
    partial_rows = grads[0]
    mats, rows_shard, width = partial_rows.shape
    n_replica = lax.axis_size("dp")
    n_shard = lax.axis_size("fsdp")
    owners = n_replica * n_shard
    cap = momentum.shape[0]
    rows_owner = rows_shard // n_replica
    reduced = lax.psum_scatter(partial_rows, "dp", scatter_dimension=1, tiled=True)
    slot_ids = jnp.arange(owners * cap, dtype=jnp.int32)
    matched = owner_slot[None, :] == slot_ids[:, None]
    holder = jnp.sum(jnp.where(matched, jnp.arange(mats, dtype=jnp.int32)[None, :], 0), axis=1)
    filled = jnp.any(matched, axis=1)
    outgoing = jnp.where(filled[:, None, None], jnp.take(reduced, holder, axis=0), 0.0)
    arrived = lax.all_to_all(
        outgoing.reshape(owners, cap, rows_owner, width),
        ("dp", "fsdp"),
        split_axis=0,
        concat_axis=0,
        tiled=True,
    )
    arrived = arrived.reshape(n_replica, n_shard, cap, rows_owner, width)
    whole = jnp.transpose(arrived, (2, 1, 0, 3, 4)).reshape(
        cap, n_shard * n_replica * rows_owner, width
    )
    buffer = MOMENT * momentum.astype(jnp.float32) + whole
    new_momentum = buffer.astype(jnp.bfloat16)
    nesterov = whole + MOMENT * buffer
    ortho = (FACTOR * orthogonalize(nesterov)).astype(jnp.bfloat16)
    leaving = jnp.transpose(
        ortho.reshape(cap, n_shard, n_replica, rows_owner, width), (2, 1, 0, 3, 4)
    )
    returned = lax.all_to_all(
        leaving.reshape(owners, cap, rows_owner, width),
        ("dp", "fsdp"),
        split_axis=0,
        concat_axis=0,
        tiled=True,
    )
    returned = returned.reshape(owners * cap, rows_owner, width)
    mine = jnp.take(returned, owner_slot, axis=0)
    updates = lax.all_gather(mine, "dp", axis=1, tiled=True)
    return (updates, new_momentum)


def here():
    d = lax.axis_index("dp")
    return d // 2, d % 2, lax.axis_index("fsdp")


def matrix_at(slots, chip, core):
    slot = (chip // 2) * 4 + core * 2 + chip % 2
    found = jnp.int32(-1)
    for j in range(4):
        found = jnp.where(slots[j] == slot, jnp.int32(j), found)
    return found


def deal(slots):
    at = [[matrix_at(slots, chip, core) for core in (0, 1)] for chip in range(4)]
    one, zero = jnp.int32(1), jnp.int32(0)
    extra = [
        jnp.where(at[q][0] >= 0, one, zero) + jnp.where(at[q][1] >= 0, one, zero) - 1
        for q in range(4)
    ]
    row = [extra[y] + extra[2 + y] for y in (0, 1)]
    out_y = [
        jnp.where((row[q % 2] > 0) & (extra[q ^ 1] < 0), one, zero) for q in range(4)
    ]
    out_x = [
        jnp.where(extra[q] - out_y[q] + out_y[q ^ 1] > 0, one, zero) for q in range(4)
    ]
    keep = [jnp.where(at[q][0] >= 0, at[q][0], at[q][1]) for q in range(4)]
    give = [jnp.where(at[q][1] >= 0, at[q][1], at[q][0]) for q in range(4)]
    matrix = [
        jnp.clip(
            jnp.where(
                out_y[q ^ 1] > 0, give[q ^ 1], jnp.where(out_x[q ^ 2] > 0, give[q ^ 2], keep[q])
            ),
            0,
            3,
        )
        for q in range(4)
    ]
    return at, out_x, out_y, matrix


def pick(values, index):
    result = values[0]
    for k in range(1, len(values)):
        result = jnp.where(index == k, values[k], result)
    return result


def sum_kernel(slots, own, other, mom, mom_other, to_x, to_y, to_d, mom_out):
    x, c, y = here()

    @pl.when(c == 1)
    def _():
        at, _, _, matrix = deal([slots[j] for j in range(4)])
        q = 2 * x + y
        for out, flip in ((to_d, 3), (to_x, 2), (to_y, 1)):
            m = pick([matrix[k ^ flip] for k in range(4)], q)
            out[...] = own[0, m] + other[0, m]
        mine = pick([at[k][1] for k in range(4)], q) >= 0

        @pl.when(mine)
        def _():
            mom_out[...] = mom[0]

        @pl.when(jnp.logical_not(mine))
        def _():
            mom_out[...] = mom_other[0]


def polynomial_step(current):
    contract = functools.partial(
        lax.dot_general, precision=lax.Precision.HIGH, preferred_element_type=jnp.float32
    )
    gram = contract(current, current, (((1,), (1,)), ((), ())))
    square = contract(gram, gram, (((1,), (0,)), ((), ())))
    poly = COEF_B * gram + COEF_C * square
    return COEF_A * current + contract(poly, current, (((1,), (0,)), ((), ())))


def first_kernel(
    steps, slots, own, other, in_x, in_y, in_d, mom, mom_other, mom_x, mom_y, new, current
):
    x, c, y = here()
    half = own.shape[2]

    @pl.when(c == 0)
    def _():
        at, out_x, out_y, matrix = deal([slots[j] for j in range(4)])
        q = 2 * x + y
        m = pick(matrix, q)
        from_y = pick([out_y[k ^ 1] for k in range(4)], q) > 0
        from_x = pick([out_x[k ^ 2] for k in range(4)], q) > 0
        from_0 = pick([at[k][0] for k in range(4)], q) >= 0
        pieces = []
        for part, start in enumerate((y * half, (1 - y) * half)):
            rows = pl.ds(pl.multiple_of(start, half), half)
            if part == 0:
                total = (own[0, m] + other[0, m]) + in_x[...]
            else:
                total = in_y[...] + in_d[...]
            held = jnp.where(from_0, mom[0, rows], mom_other[0, rows])
            held = jnp.where(from_x, mom_x[rows], held)
            held = jnp.where(from_y, mom_y[rows], held)
            buffer = MOMENT * held.astype(jnp.float32) + total
            new[rows] = buffer.astype(jnp.bfloat16)
            pieces.append(total + MOMENT * buffer)
        nesterov = jnp.concatenate(pieces, axis=0)
        norm = jnp.sqrt(jnp.sum(nesterov * nesterov))
        value = nesterov / (norm + 1e-07)
        for _ in range(steps):
            value = polynomial_step(value)
        current[...] = value


def middle_kernel(steps, before, after):
    _, c, _ = here()

    @pl.when(c == 0)
    def _():
        value = before[...]
        for _ in range(steps):
            value = polynomial_step(value)
        after[...] = value


def last_kernel(steps, before, mine, others):
    _, c, _ = here()
    half = mine.shape[0]

    @pl.when(c == 0)
    def _():
        value = before[...]
        for _ in range(steps):
            value = polynomial_step(value)
        value = (FACTOR * value).astype(jnp.bfloat16)
        mine[...] = value[:half]
        others[...] = value[half:]


def back_kernel(slots, new_x, new_y, back):
    x, c, y = here()

    @pl.when(c == 1)
    def _():
        _, out_x, _, _ = deal([slots[j] for j in range(4)])
        along_x = pick(out_x, 2 * x + y) > 0
        back[...] = jnp.where(along_x, new_x[...], new_y[...])


def momentum_kernel(slots, mom, new, back, new_in, out):
    x, c, y = here()
    at, out_x, out_y, _ = deal([slots[j] for j in range(4)])
    q = 2 * x + y
    at_0 = pick([at[k][0] for k in range(4)], q) >= 0
    at_1 = pick([at[k][1] for k in range(4)], q) >= 0
    gone = pick([out_x[k] + out_y[k] for k in range(4)], q) > 0
    mine = jnp.where(c == 0, at_0, at_1)
    away = jnp.where(c == 0, gone & jnp.logical_not(at_1), gone)

    @pl.when(jnp.logical_not(mine))
    def _():
        out[0] = (MOMENT * mom[0].astype(jnp.float32)).astype(jnp.bfloat16)

    @pl.when(mine & (c == 0) & away)
    def _():
        out[0] = new_in[...]

    @pl.when(mine & (c == 0) & jnp.logical_not(away))
    def _():
        out[0] = new[...]

    @pl.when(mine & (c == 1) & away)
    def _():
        out[0] = back[...]

    @pl.when(mine & (c == 1) & jnp.logical_not(away))
    def _():
        out[0] = new_in[...]


def gather_kernel(slots, mine, up_l, up_x, up_y, up_d, in_x, in_y, in_d, out, sems):
    x, c, y = here()
    _, _, _, matrix = deal([slots[j] for j in range(4)])
    q = 2 * x + y
    for core, sources in ((0, (mine, in_y, in_x, in_d)), (1, (up_l, up_y, up_x, up_d))):

        @pl.when(c == core)
        def _():
            copies = []
            for flip, source in enumerate(sources):
                m = pick([matrix[k ^ flip] for k in range(4)], q)
                copy = pltpu.make_async_copy(source, out.at[m], sems.at[flip])
                copy.start()
                copies.append(copy)
            for copy in copies:
                copy.wait()


def chip_device(x, c, y):
    return (2 * x + c) * 2 + y


CHIPS = [(x, y) for x in (0, 1) for y in (0, 1)]


def swap_cores(value):
    pairs = [
        (chip_device(x, c, y), chip_device(x, 1 - c, y)) for x, y in CHIPS for c in (0, 1)
    ]
    return lax.ppermute(value, AXES, pairs)


def across(value, sender, flip_x, flip_y):
    pairs = [
        (chip_device(x, sender, y), chip_device(x ^ flip_x, 1 - sender, y ^ flip_y))
        for x, y in CHIPS
    ]
    pairs += [(chip_device(x, 1 - sender, y), chip_device(x, sender, y)) for x, y in CHIPS]
    return lax.ppermute(value, AXES, pairs)


def between_ones(value, flip_x, flip_y):
    pairs = [
        (chip_device(x, 1, y), chip_device(x ^ flip_x, 1, y ^ flip_y)) for x, y in CHIPS
    ]
    pairs += [(chip_device(x, 0, y), chip_device(x, 0, y)) for x, y in CHIPS]
    return lax.ppermute(value, AXES, pairs)


def run(kernel, in_specs, out_shapes, out_specs=None, scratch=(), flops=0, moved=0):
    return pl.pallas_call(
        kernel,
        in_specs=in_specs,
        out_shape=out_shapes,
        out_specs=out_specs if out_specs is not None else [VMEM] * len(out_shapes),
        scratch_shapes=list(scratch),
        compiler_params=pltpu.CompilerParams(vmem_limit_bytes=24 * 2**20),
        cost_estimate=pl.CostEstimate(flops=flops, bytes_accessed=moved, transcendentals=0),
    )


def per_device_chips(grads, owner_slot, momentum):
    _, mats, half, width = grads.shape
    rows = momentum.shape[1]
    f32, bf16 = jnp.float32, jnp.bfloat16
    piece = jax.ShapeDtypeStruct((half, width), f32)
    whole = jax.ShapeDtypeStruct((rows, width), f32)
    moment = jax.ShapeDtypeStruct((rows, width), bf16)
    update = jax.ShapeDtypeStruct((half, width), bf16)
    step_flops = 6 * (2 * rows * rows * width * 2 + 2 * rows * rows * rows)

    grads_other = swap_cores(grads)
    mom_other = swap_cores(momentum)
    to_x, to_y, to_d, mom_out = run(
        sum_kernel, [SMEM] + [VMEM] * 4, [piece, piece, piece, moment], moved=3 * 2**20
    )(owner_slot, grads, grads_other, momentum, mom_other)
    in_d = across(to_d, 1, 1, 1)
    in_x = across(to_x, 1, 1, 0)
    in_y = across(to_y, 1, 0, 1)
    mom_x = across(mom_out, 1, 1, 0)
    mom_y = across(mom_out, 1, 0, 1)
    new, current = run(
        functools.partial(first_kernel, 1),
        [SMEM] + [VMEM] * 9,
        [moment, whole],
        flops=step_flops,
        moved=3 * 2**20,
    )(owner_slot, grads, grads_other, in_x, in_y, in_d, momentum, mom_other, mom_x, mom_y)
    new_l = swap_cores(new)
    (current,) = run(
        functools.partial(middle_kernel, 2), [VMEM], [whole], flops=2 * step_flops, moved=2**20
    )(current)
    new_x = between_ones(new_l, 1, 0)
    new_y = between_ones(new_l, 0, 1)
    mine, others = run(
        functools.partial(last_kernel, 2), [VMEM], [update, update], flops=2 * step_flops, moved=2**20
    )(current)
    up_d = across(others, 0, 1, 1)
    up_x = across(mine, 0, 1, 0)
    up_y = across(others, 0, 0, 1)
    up_l = swap_cores(mine)
    (back,) = run(back_kernel, [SMEM, VMEM, VMEM], [moment], moved=2**19)(owner_slot, new_x, new_y)
    back_in = swap_cores(back)
    new_in = jnp.where(lax.axis_index("dp") % 2 == 0, back_in, new_l)
    (new_momentum,) = run(
        momentum_kernel,
        [SMEM] + [VMEM] * 4,
        [jax.ShapeDtypeStruct(momentum.shape, bf16)],
        moved=2**19,
    )(owner_slot, momentum, new, back, new_in)
    over_d, over_x, over_y = swap_cores(up_d), swap_cores(up_x), swap_cores(up_y)
    (updates,) = run(
        gather_kernel,
        [SMEM] + [VMEM] * 8,
        [jax.ShapeDtypeStruct((mats, half, width), bf16)],
        out_specs=[ANY],
        scratch=[pltpu.SemaphoreType.DMA((4,))],
        moved=2**20,
    )(owner_slot, mine, up_l, up_x, up_y, up_d, over_x, over_y, over_d)
    return (updates, new_momentum)


def solution(mesh):
    placed = (P("dp", "expert", "fsdp", None), P("expert"), P(("dp", "expert", "fsdp"), None, None))
    n_replica, n_shard = mesh.shape["dp"], mesh.shape["fsdp"]

    def per_device(grads, owner_slot, momentum):
        mats, cap = grads.shape[1], momentum.shape[0]
        if (n_replica, n_shard, mats, cap) == (4, 2, 4, 1):
            return per_device_chips(grads, owner_slot, momentum)
        return per_device_general(grads, owner_slot, momentum)

    return jax.shard_map(
        per_device,
        mesh=mesh,
        in_specs=placed,
        out_specs=(P("expert", "fsdp", None), P(("dp", "expert", "fsdp"), None, None)),
        check_vma=False,
    )
```

```python
import functools
import math

import jax
import jax.numpy as jnp
from jax import lax
from jax.experimental import pallas as pl
from jax.experimental.pallas import tpu as pltpu
from jax.sharding import PartitionSpec as P

R = 256
C = 512
ITERS = 5


COEF_A = 3.4445
COEF_B = -4.775
COEF_C = 2.0315
MOMENT = 0.95
FACTOR = 0.2 * math.sqrt(max(R, C))

AXES = ("dp", "fsdp")
VMEM = pl.BlockSpec(memory_space=pltpu.VMEM)
ANY = pl.BlockSpec(memory_space=pl.ANY)


def orthogonalize(stack):
    norms = jnp.sqrt(jnp.sum(stack * stack, axis=(1, 2), keepdims=True))
    current = stack / (norms + 1e-07)
    for step in range(ITERS):
        gram = jnp.einsum("krc,ksc->krs", current, current, precision=lax.Precision.HIGHEST)
        square = jnp.einsum("krs,kst->krt", gram, gram, precision=lax.Precision.HIGHEST)
        poly = COEF_B * gram + COEF_C * square
        current = COEF_A * current + jnp.einsum(
            "krs,ksc->krc", poly, current, precision=lax.Precision.HIGHEST
        )
    return current


def per_device_general(grads, owner_slot, momentum):
    partial_rows = grads[0]
    mats, rows_shard, width = partial_rows.shape
    n_replica = lax.axis_size("dp")
    n_shard = lax.axis_size("fsdp")
    owners = n_replica * n_shard
    cap = momentum.shape[0]
    rows_owner = rows_shard // n_replica
    reduced = lax.psum_scatter(partial_rows, "dp", scatter_dimension=1, tiled=True)
    slot_ids = jnp.arange(owners * cap, dtype=jnp.int32)
    matched = owner_slot[None, :] == slot_ids[:, None]
    holder = jnp.sum(jnp.where(matched, jnp.arange(mats, dtype=jnp.int32)[None, :], 0), axis=1)
    filled = jnp.any(matched, axis=1)
    outgoing = jnp.where(filled[:, None, None], jnp.take(reduced, holder, axis=0), 0.0)
    arrived = lax.all_to_all(
        outgoing.reshape(owners, cap, rows_owner, width),
        ("dp", "fsdp"),
        split_axis=0,
        concat_axis=0,
        tiled=True,
    )
    arrived = arrived.reshape(n_replica, n_shard, cap, rows_owner, width)
    whole = jnp.transpose(arrived, (2, 1, 0, 3, 4)).reshape(
        cap, n_shard * n_replica * rows_owner, width
    )
    buffer = MOMENT * momentum.astype(jnp.float32) + whole
    new_momentum = buffer.astype(jnp.bfloat16)
    nesterov = whole + MOMENT * buffer
    ortho = (FACTOR * orthogonalize(nesterov)).astype(jnp.bfloat16)
    leaving = jnp.transpose(
        ortho.reshape(cap, n_shard, n_replica, rows_owner, width), (2, 1, 0, 3, 4)
    )
    returned = lax.all_to_all(
        leaving.reshape(owners, cap, rows_owner, width),
        ("dp", "fsdp"),
        split_axis=0,
        concat_axis=0,
        tiled=True,
    )
    returned = returned.reshape(owners * cap, rows_owner, width)
    mine = jnp.take(returned, owner_slot, axis=0)
    updates = lax.all_gather(mine, "dp", axis=1, tiled=True)
    return (updates, new_momentum)


def here():
    d = lax.axis_index("dp")
    return d // 2, d % 2, lax.axis_index("fsdp")


def matrix_at(slots, chip, core):
    slot = (chip // 2) * 4 + core * 2 + chip % 2
    found = jnp.int32(-1)
    for j in range(4):
        found = jnp.where(slots[j] == slot, jnp.int32(j), found)
    return found


def deal(slots):
    at = [[matrix_at(slots, chip, core) for core in (0, 1)] for chip in range(4)]
    one, zero = jnp.int32(1), jnp.int32(0)
    extra = [
        jnp.where(at[q][0] >= 0, one, zero) + jnp.where(at[q][1] >= 0, one, zero) - 1
        for q in range(4)
    ]
    row = [extra[y] + extra[2 + y] for y in (0, 1)]
    out_y = [
        jnp.where((row[q % 2] > 0) & (extra[q ^ 1] < 0), one, zero) for q in range(4)
    ]
    out_x = [
        jnp.where(extra[q] - out_y[q] + out_y[q ^ 1] > 0, one, zero) for q in range(4)
    ]
    keep = [jnp.where(at[q][0] >= 0, at[q][0], at[q][1]) for q in range(4)]
    give = [jnp.where(at[q][1] >= 0, at[q][1], at[q][0]) for q in range(4)]
    matrix = [
        jnp.clip(
            jnp.where(
                out_y[q ^ 1] > 0, give[q ^ 1], jnp.where(out_x[q ^ 2] > 0, give[q ^ 2], keep[q])
            ),
            0,
            3,
        )
        for q in range(4)
    ]
    return at, out_x, out_y, matrix


def pick(values, index):
    result = values[0]
    for k in range(1, len(values)):
        result = jnp.where(index == k, values[k], result)
    return result


def load_kernel(grads, momentum, slots, grads_near, momentum_near, plan, slots_near, sems):
    copies = [
        pltpu.make_async_copy(source, target, sems.at[k])
        for k, (source, target) in enumerate(
            ((slots, slots_near), (momentum.at[0], momentum_near), (grads.at[0], grads_near))
        )
    ]
    for copy in copies:
        copy.start()
    copies[0].wait()
    x, c, y = here()
    at, out_x, out_y, matrix = deal([slots_near[j] for j in range(4)])
    q = 2 * x + y
    one, zero = jnp.int32(1), jnp.int32(0)
    at_0 = pick([at[k][0] for k in range(4)], q) >= 0
    at_1 = pick([at[k][1] for k in range(4)], q) >= 0
    leaves_x = pick(out_x, q)
    leaves_y = pick(out_y, q)
    comes_x = pick([out_x[k ^ 2] for k in range(4)], q) > 0
    comes_y = pick([out_y[k ^ 1] for k in range(4)], q) > 0
    mine = jnp.where(c == 0, at_0, at_1)
    away = jnp.where((c == 1) | jnp.logical_not(at_1), leaves_x + 2 * leaves_y, zero)
    entries = [pick([matrix[k ^ flip] for k in range(4)], q) for flip in range(4)]
    entries.append(jnp.where(comes_y, 3, jnp.where(comes_x, 2, jnp.where(at_0, zero, one))))
    entries.append(jnp.where(at_1, one, zero))
    entries.append(jnp.where(mine, one + away, zero))
    entries.append(leaves_x)
    row = lax.broadcasted_iota(jnp.int32, plan.shape, 0)
    table = jnp.zeros(plan.shape, jnp.int32)
    for k, entry in enumerate(entries):
        table = jnp.where(row == k, entry, table)
    plan[...] = table
    copies[1].wait()
    copies[2].wait()


SOURCE, GIVER, SLOT, LEAVES_X = 4, 5, 6, 7


def give_kernel(plan, mom, mom_other, mom_out):
    _, c, _ = here()

    @pl.when(c == 1)
    def _():
        mine = plan[GIVER, 0] == 1
        mom_out[...] = jnp.where(mine, mom[...], mom_other[0])


def sum_kernel(plan, own, other, to_d, to_x, to_y):
    _, c, _ = here()

    @pl.when(c == 1)
    def _():
        for out, flip in ((to_d, 3), (to_x, 2), (to_y, 1)):
            m = plan[flip, 0]
            out[...] = own[m] + other[0, m]


def polynomial_step(current):
    contract = functools.partial(
        lax.dot_general, precision=lax.Precision.HIGH, preferred_element_type=jnp.float32
    )
    gram = contract(current, current, (((1,), (1,)), ((), ())))
    square = contract(gram, gram, (((1,), (0,)), ((), ())))
    poly = COEF_B * gram + COEF_C * square
    return COEF_A * current + contract(poly, current, (((1,), (0,)), ((), ())))


def nesterov_kernel(
    plan, own, other, in_x, in_y, in_d, mom, mom_other, mom_x, mom_y, new, current
):
    _, c, y = here()
    half = own.shape[1]

    @pl.when(c == 0)
    def _():
        m = plan[0, 0]
        source = plan[SOURCE, 0]
        squares = jnp.float32(0)
        pieces = []
        for part, start in enumerate((y * half, (1 - y) * half)):
            rows = pl.ds(pl.multiple_of(start, half), half)
            if part == 0:
                total = (own[m] + other[0, m]) + in_x[...]
            else:
                total = in_y[...] + in_d[...]
            held = pick([mom[rows], mom_other[0, rows], mom_x[rows], mom_y[rows]], source)
            buffer = MOMENT * held.astype(jnp.float32) + total
            new[rows] = buffer.astype(jnp.bfloat16)
            piece = total + MOMENT * buffer
            squares = squares + jnp.sum(piece * piece)
            pieces.append(piece)
        norm = jnp.sqrt(squares) + 1e-07
        for part in (0, 1):
            current[part * half : (part + 1) * half] = pieces[part] / norm


def middle_kernel(steps, before, after):
    _, c, _ = here()

    @pl.when(c == 0)
    def _():
        value = before[...]
        for _ in range(steps):
            value = polynomial_step(value)
        after[...] = value


def last_kernel(steps, before, others, mine):
    _, c, _ = here()
    half = mine.shape[0]

    @pl.when(c == 0)
    def _():
        value = before[...]
        for _ in range(steps):
            value = polynomial_step(value)
        value = (FACTOR * value).astype(jnp.bfloat16)
        mine[...] = value[:half]
        others[...] = value[half:]


def back_kernel(plan, mom, new_l, new_x, new_y, back, hold):
    _, c, _ = here()

    @pl.when(c == 1)
    def _():
        back[...] = jnp.where(plan[LEAVES_X, 0] == 1, new_x[...], new_y[...])

    faded = (MOMENT * mom[...].astype(jnp.float32)).astype(jnp.bfloat16)
    slot = jnp.where(c == 1, plan[SLOT, 0], 0)
    hold[...] = pick([faded, new_l[...], new_x[...], new_y[...]], slot)


def finish_kernel(
    plan, mine, up_l, up_x, up_y, up_d, in_x, in_y, in_d, new, back, hold, updates, moment, sems
):
    _, c, _ = here()
    for core, sources in ((0, (mine, in_y, in_x, in_d)), (1, (up_l, up_y, up_x, up_d))):

        @pl.when(c == core)
        def _():
            for flip, source in enumerate(sources):
                m = plan[flip, 0]
                pltpu.make_async_copy(source, updates.at[m], sems.at[flip]).start()

    slot = plan[SLOT, 0]
    held = (c == 1) | (slot == 0)
    for chosen, source in (
        (held, hold),
        (jnp.logical_not(held) & (slot == 1), new),
        (jnp.logical_not(held) & (slot > 1), back),
    ):

        @pl.when(chosen)
        def _():
            pltpu.make_async_copy(source, moment.at[0], sems.at[4]).start()

    for flip in range(4):
        pltpu.make_async_copy(mine, updates.at[flip], sems.at[flip]).wait()
    pltpu.make_async_copy(hold, moment.at[0], sems.at[4]).wait()


def chip_device(x, c, y):
    return (2 * x + c) * 2 + y


CHIPS = [(x, y) for x in (0, 1) for y in (0, 1)]


def swap_cores(value):
    pairs = [
        (chip_device(x, c, y), chip_device(x, 1 - c, y)) for x, y in CHIPS for c in (0, 1)
    ]
    return lax.ppermute(value, AXES, pairs)


def across(value, sender, flip_x, flip_y):
    pairs = [
        (chip_device(x, sender, y), chip_device(x ^ flip_x, 1 - sender, y ^ flip_y))
        for x, y in CHIPS
    ]
    pairs += [(chip_device(x, 1 - sender, y), chip_device(x, sender, y)) for x, y in CHIPS]
    return lax.ppermute(value, AXES, pairs)


def run(kernel, in_specs, out_shapes, out_specs=None, scratch=(), flops=0, moved=0):
    return pl.pallas_call(
        kernel,
        in_specs=in_specs,
        out_shape=out_shapes,
        out_specs=out_specs if out_specs is not None else [VMEM] * len(out_shapes),
        scratch_shapes=list(scratch),
        compiler_params=pltpu.CompilerParams(vmem_limit_bytes=24 * 2**20),
        cost_estimate=pl.CostEstimate(flops=flops, bytes_accessed=moved, transcendentals=0),
    )


def per_device_chips(grads, owner_slot, momentum):
    _, mats, half, width = grads.shape
    rows = momentum.shape[1]
    f32, bf16 = jnp.float32, jnp.bfloat16
    piece = jax.ShapeDtypeStruct((half, width), f32)
    whole = jax.ShapeDtypeStruct((rows, width), f32)
    moment = jax.ShapeDtypeStruct((rows, width), bf16)
    update = jax.ShapeDtypeStruct((half, width), bf16)
    step_flops = 6 * (2 * rows * rows * width * 2 + 2 * rows * rows * rows)

    near = jax.ShapeDtypeStruct((mats, half, width), f32)
    table = jax.ShapeDtypeStruct((8, 128), jnp.int32)

    mom_other = swap_cores(momentum)
    grads_other = swap_cores(grads)
    own, mom, plan = run(
        load_kernel,
        [ANY] * 3,
        [near, moment, table],
        scratch=[pltpu.SMEM((mats,), jnp.int32), pltpu.SemaphoreType.DMA((3,))],
        moved=2**21,
    )(*(pltpu.with_memory_space_constraint(a, pltpu.HBM) for a in (grads, momentum, owner_slot)))
    (mom_out,) = run(give_kernel, [VMEM] * 3, [moment], moved=2**18)(plan, mom, mom_other)
    mom_x = across(mom_out, 1, 1, 0)
    mom_y = across(mom_out, 1, 0, 1)
    to_d, to_x, to_y = run(sum_kernel, [VMEM] * 3, [piece, piece, piece], moved=2**20)(
        plan, own, grads_other
    )
    in_d = across(to_d, 1, 1, 1)
    in_x = across(to_x, 1, 1, 0)
    in_y = across(to_y, 1, 0, 1)
    new, current = run(nesterov_kernel, [VMEM] * 10, [moment, whole], moved=2**20)(
        plan, own, grads_other, in_x, in_y, in_d, mom, mom_other, mom_x, mom_y
    )
    new_x = across(new, 0, 1, 0)
    (current,) = run(
        functools.partial(middle_kernel, 2), [VMEM], [whole], flops=2 * step_flops, moved=2**20
    )(current)
    new, current = lax.optimization_barrier((new, current))
    new_y = across(new, 0, 0, 1)
    new_l = swap_cores(new)
    others, mine = run(
        functools.partial(last_kernel, 3), [VMEM], [update, update], flops=3 * step_flops, moved=2**20
    )(current)
    up_d = across(others, 0, 1, 1)
    up_x = across(mine, 0, 1, 0)
    up_y = across(others, 0, 0, 1)
    up_l = swap_cores(mine)
    back, hold = run(back_kernel, [VMEM] * 5, [moment, moment], moved=2**19)(
        plan, mom, new_l, new_x, new_y
    )
    back_in = swap_cores(back)
    over_d, over_x, over_y = swap_cores(up_d), swap_cores(up_x), swap_cores(up_y)
    updates, new_momentum = run(
        finish_kernel,
        [VMEM] * 12,
        [jax.ShapeDtypeStruct((mats, half, width), bf16), jax.ShapeDtypeStruct(momentum.shape, bf16)],
        out_specs=[ANY, ANY],
        scratch=[pltpu.SemaphoreType.DMA((5,))],
        moved=2**20,
    )(plan, mine, up_l, up_x, up_y, up_d, over_x, over_y, over_d, new, back_in, hold)
    return (updates, new_momentum)


def solution(mesh):
    placed = (P("dp", "expert", "fsdp", None), P("expert"), P(("dp", "expert", "fsdp"), None, None))
    n_replica, n_shard = mesh.shape["dp"], mesh.shape["fsdp"]

    def per_device(grads, owner_slot, momentum):
        mats, cap = grads.shape[1], momentum.shape[0]
        if (n_replica, n_shard, mats, cap) == (4, 2, 4, 1):
            return per_device_chips(grads, owner_slot, momentum)
        return per_device_general(grads, owner_slot, momentum)

    return jax.shard_map(
        per_device,
        mesh=mesh,
        in_specs=placed,
        out_specs=(P("expert", "fsdp", None), P(("dp", "expert", "fsdp"), None, None)),
        check_vma=False,
    )
```

```python
import functools
import math

import jax
import jax.numpy as jnp
from jax import lax
from jax.experimental import pallas as pl
from jax.experimental.pallas import tpu as pltpu
from jax.sharding import PartitionSpec as P

R = 256
C = 512
ITERS = 5


COEF_A = 3.4445
COEF_B = -4.775
COEF_C = 2.0315
MOMENT = 0.95
FACTOR = 0.2 * math.sqrt(max(R, C))

AXES = ("dp", "fsdp")
VMEM = pl.BlockSpec(memory_space=pltpu.VMEM)
ANY = pl.BlockSpec(memory_space=pl.ANY)


def orthogonalize(stack):
    norms = jnp.sqrt(jnp.sum(stack * stack, axis=(1, 2), keepdims=True))
    current = stack / (norms + 1e-07)
    for step in range(ITERS):
        gram = jnp.einsum("krc,ksc->krs", current, current, precision=lax.Precision.HIGHEST)
        square = jnp.einsum("krs,kst->krt", gram, gram, precision=lax.Precision.HIGHEST)
        poly = COEF_B * gram + COEF_C * square
        current = COEF_A * current + jnp.einsum(
            "krs,ksc->krc", poly, current, precision=lax.Precision.HIGHEST
        )
    return current


def per_device_general(grads, owner_slot, momentum):
    partial_rows = grads[0]
    mats, rows_shard, width = partial_rows.shape
    n_replica = lax.axis_size("dp")
    n_shard = lax.axis_size("fsdp")
    owners = n_replica * n_shard
    cap = momentum.shape[0]
    rows_owner = rows_shard // n_replica
    reduced = lax.psum_scatter(partial_rows, "dp", scatter_dimension=1, tiled=True)
    slot_ids = jnp.arange(owners * cap, dtype=jnp.int32)
    matched = owner_slot[None, :] == slot_ids[:, None]
    holder = jnp.sum(jnp.where(matched, jnp.arange(mats, dtype=jnp.int32)[None, :], 0), axis=1)
    filled = jnp.any(matched, axis=1)
    outgoing = jnp.where(filled[:, None, None], jnp.take(reduced, holder, axis=0), 0.0)
    arrived = lax.all_to_all(
        outgoing.reshape(owners, cap, rows_owner, width),
        ("dp", "fsdp"),
        split_axis=0,
        concat_axis=0,
        tiled=True,
    )
    arrived = arrived.reshape(n_replica, n_shard, cap, rows_owner, width)
    whole = jnp.transpose(arrived, (2, 1, 0, 3, 4)).reshape(
        cap, n_shard * n_replica * rows_owner, width
    )
    buffer = MOMENT * momentum.astype(jnp.float32) + whole
    new_momentum = buffer.astype(jnp.bfloat16)
    nesterov = whole + MOMENT * buffer
    ortho = (FACTOR * orthogonalize(nesterov)).astype(jnp.bfloat16)
    leaving = jnp.transpose(
        ortho.reshape(cap, n_shard, n_replica, rows_owner, width), (2, 1, 0, 3, 4)
    )
    returned = lax.all_to_all(
        leaving.reshape(owners, cap, rows_owner, width),
        ("dp", "fsdp"),
        split_axis=0,
        concat_axis=0,
        tiled=True,
    )
    returned = returned.reshape(owners * cap, rows_owner, width)
    mine = jnp.take(returned, owner_slot, axis=0)
    updates = lax.all_gather(mine, "dp", axis=1, tiled=True)
    return (updates, new_momentum)


def here():
    d = lax.axis_index("dp")
    return d // 2, d % 2, lax.axis_index("fsdp")


def matrix_at(slots, chip, core):
    slot = (chip // 2) * 4 + core * 2 + chip % 2
    found = jnp.int32(-1)
    for j in range(4):
        found = jnp.where(slots[j] == slot, jnp.int32(j), found)
    return found


def deal(slots):
    at = [[matrix_at(slots, chip, core) for core in (0, 1)] for chip in range(4)]
    one, zero = jnp.int32(1), jnp.int32(0)
    extra = [
        jnp.where(at[q][0] >= 0, one, zero) + jnp.where(at[q][1] >= 0, one, zero) - 1
        for q in range(4)
    ]
    row = [extra[y] + extra[2 + y] for y in (0, 1)]
    out_y = [
        jnp.where((row[q % 2] > 0) & (extra[q ^ 1] < 0), one, zero) for q in range(4)
    ]
    out_x = [
        jnp.where(extra[q] - out_y[q] + out_y[q ^ 1] > 0, one, zero) for q in range(4)
    ]
    keep = [jnp.where(at[q][0] >= 0, at[q][0], at[q][1]) for q in range(4)]
    give = [jnp.where(at[q][1] >= 0, at[q][1], at[q][0]) for q in range(4)]
    matrix = [
        jnp.clip(
            jnp.where(
                out_y[q ^ 1] > 0, give[q ^ 1], jnp.where(out_x[q ^ 2] > 0, give[q ^ 2], keep[q])
            ),
            0,
            3,
        )
        for q in range(4)
    ]
    return at, out_x, out_y, matrix


def pick(values, index):
    result = values[0]
    for k in range(1, len(values)):
        result = jnp.where(index == k, values[k], result)
    return result


def load_kernel(grads, momentum, slots, grads_near, momentum_near, plan, slots_near, sems):
    copies = [
        pltpu.make_async_copy(source, target, sems.at[k])
        for k, (source, target) in enumerate(
            ((slots, slots_near), (momentum.at[0], momentum_near), (grads.at[0], grads_near))
        )
    ]
    for copy in copies:
        copy.start()
    copies[0].wait()
    x, c, y = here()
    at, out_x, out_y, matrix = deal([slots_near[j] for j in range(4)])
    q = 2 * x + y
    one, zero = jnp.int32(1), jnp.int32(0)
    at_0 = pick([at[k][0] for k in range(4)], q) >= 0
    at_1 = pick([at[k][1] for k in range(4)], q) >= 0
    leaves_x = pick(out_x, q)
    leaves_y = pick(out_y, q)
    comes_x = pick([out_x[k ^ 2] for k in range(4)], q) > 0
    comes_y = pick([out_y[k ^ 1] for k in range(4)], q) > 0
    mine = jnp.where(c == 0, at_0, at_1)
    away = jnp.where((c == 1) | jnp.logical_not(at_1), leaves_x + 2 * leaves_y, zero)
    entries = [pick([matrix[k ^ flip] for k in range(4)], q) for flip in range(4)]
    entries.append(jnp.where(comes_y, 3, jnp.where(comes_x, 2, jnp.where(at_0, zero, one))))
    entries.append(jnp.where(at_1, one, zero))
    entries.append(jnp.where(mine, one + away, zero))
    entries.append(leaves_x)
    row = lax.broadcasted_iota(jnp.int32, plan.shape, 0)
    table = jnp.zeros(plan.shape, jnp.int32)
    for k, entry in enumerate(entries):
        table = jnp.where(row == k, entry, table)
    plan[...] = table
    copies[1].wait()
    copies[2].wait()


SOURCE, GIVER, SLOT, LEAVES_X = 4, 5, 6, 7


def give_kernel(plan, mom, mom_other, mom_out):
    _, c, _ = here()

    @pl.when(c == 1)
    def _():
        mine = plan[GIVER, 0] == 1
        mom_out[...] = jnp.where(mine, mom[...], mom_other[0])


def sum_kernel(plan, own, other, to_d, to_x, to_y):
    _, c, _ = here()

    @pl.when(c == 1)
    def _():
        for out, flip in ((to_d, 3), (to_x, 2), (to_y, 1)):
            m = plan[flip, 0]
            out[...] = own[m] + other[0, m]


def parts_of(value):
    high = value.astype(jnp.bfloat16)
    return high, (value - high.astype(jnp.float32)).astype(jnp.bfloat16)


def polynomial_step(current):
    dot = functools.partial(lax.dot_general, preferred_element_type=jnp.float32)
    plain, turned = (((1,), (0,)), ((), ())), (((1,), (1,)), ((), ()))
    high, low = parts_of(current)
    mixed = dot(high, low, turned)
    gram = dot(high, high, turned) + (mixed + mixed.T)
    gram_high, gram_low = parts_of(gram)
    rows = current.shape[0] // 2
    blocks = []
    for k in (0, 1):
        block = slice(k * rows, (k + 1) * rows)
        square = dot(gram_high[block], gram_high, plain) + (
            dot(gram_high[block], gram_low, plain) + dot(gram_low[block], gram_high, plain)
        )
        poly_high, poly_low = parts_of(COEF_B * gram[block] + COEF_C * square)
        change = dot(poly_high, high, plain) + (
            dot(poly_high, low, plain) + dot(poly_low, high, plain)
        )
        blocks.append(COEF_A * current[block] + change)
    return jnp.concatenate(blocks, axis=0)


def nesterov_kernel(
    plan, mom_other, mom_x, mom_y, other, in_d, in_x, in_y, own, mom, new, current
):
    _, c, y = here()
    half = own.shape[1]

    @pl.when(c == 0)
    def _():
        m = plan[0, 0]
        source = plan[SOURCE, 0]
        squares = jnp.float32(0)
        pieces = []
        for part, start in enumerate((y * half, (1 - y) * half)):
            rows = pl.ds(pl.multiple_of(start, half), half)
            if part == 0:
                total = (own[m] + other[0, m]) + in_x[...]
            else:
                total = in_y[...] + in_d[...]
            held = pick([mom[rows], mom_other[0, rows], mom_x[rows], mom_y[rows]], source)
            buffer = MOMENT * held.astype(jnp.float32) + total
            new[rows] = buffer.astype(jnp.bfloat16)
            piece = total + MOMENT * buffer
            squares = squares + jnp.sum(piece * piece)
            pieces.append(piece)
        norm = jnp.sqrt(squares) + 1e-07
        for part in (0, 1):
            current[part * half : (part + 1) * half] = pieces[part] / norm


def orthogonalize_kernel(start, others, mine):
    _, c, _ = here()
    half = mine.shape[0]

    @pl.when(c == 0)
    def _():
        value = start[...]
        for _ in range(ITERS):
            value = polynomial_step(value)
        value = (FACTOR * value).astype(jnp.bfloat16)
        mine[...] = value[:half]
        others[...] = value[half:]


def back_kernel(plan, mom, new_x, new_y, new_l, back, hold):
    _, c, _ = here()

    @pl.when(c == 1)
    def _():
        back[...] = jnp.where(plan[LEAVES_X, 0] == 1, new_x[...], new_y[...])

    faded = (MOMENT * mom[...].astype(jnp.float32)).astype(jnp.bfloat16)
    slot = jnp.where(c == 1, plan[SLOT, 0], 0)
    hold[...] = pick([faded, new_l[...], new_x[...], new_y[...]], slot)


def finish_kernel(
    plan, new, back, hold, up_x, up_y, up_d, up_l, in_x, in_y, in_d, mine, updates, moment, sems
):
    _, c, _ = here()
    for core, sources in ((0, (mine, in_y, in_x, in_d)), (1, (up_l, up_y, up_x, up_d))):

        @pl.when(c == core)
        def _():
            for flip, source in enumerate(sources):
                m = plan[flip, 0]
                pltpu.make_async_copy(source, updates.at[m], sems.at[flip]).start()

    slot = plan[SLOT, 0]
    held = (c == 1) | (slot == 0)
    for chosen, source in (
        (held, hold),
        (jnp.logical_not(held) & (slot == 1), new),
        (jnp.logical_not(held) & (slot > 1), back),
    ):

        @pl.when(chosen)
        def _():
            pltpu.make_async_copy(source, moment.at[0], sems.at[4]).start()

    for flip in range(4):
        pltpu.make_async_copy(mine, updates.at[flip], sems.at[flip]).wait()
    pltpu.make_async_copy(hold, moment.at[0], sems.at[4]).wait()


def chip_device(x, c, y):
    return (2 * x + c) * 2 + y


CHIPS = [(x, y) for x in (0, 1) for y in (0, 1)]


def swap_cores(value):
    pairs = [
        (chip_device(x, c, y), chip_device(x, 1 - c, y)) for x, y in CHIPS for c in (0, 1)
    ]
    return lax.ppermute(value, AXES, pairs)


def across(value, sender, flip_x, flip_y):
    pairs = [
        (chip_device(x, sender, y), chip_device(x ^ flip_x, 1 - sender, y ^ flip_y))
        for x, y in CHIPS
    ]
    pairs += [(chip_device(x, 1 - sender, y), chip_device(x, sender, y)) for x, y in CHIPS]
    return lax.ppermute(value, AXES, pairs)


def run(kernel, in_specs, out_shapes, out_specs=None, scratch=(), flops=0, moved=0):
    return pl.pallas_call(
        kernel,
        in_specs=in_specs,
        out_shape=out_shapes,
        out_specs=out_specs if out_specs is not None else [VMEM] * len(out_shapes),
        scratch_shapes=list(scratch),
        compiler_params=pltpu.CompilerParams(vmem_limit_bytes=24 * 2**20),
        cost_estimate=pl.CostEstimate(flops=flops, bytes_accessed=moved, transcendentals=0),
    )


def per_device_chips(grads, owner_slot, momentum):
    _, mats, half, width = grads.shape
    rows = momentum.shape[1]
    f32, bf16 = jnp.float32, jnp.bfloat16
    piece = jax.ShapeDtypeStruct((half, width), f32)
    whole = jax.ShapeDtypeStruct((rows, width), f32)
    moment = jax.ShapeDtypeStruct((rows, width), bf16)
    update = jax.ShapeDtypeStruct((half, width), bf16)

    near = jax.ShapeDtypeStruct((mats, half, width), f32)
    table = jax.ShapeDtypeStruct((8, 128), jnp.int32)

    mom_other = swap_cores(momentum)
    far = functools.partial(pltpu.with_memory_space_constraint, memory_space=pltpu.HBM)
    own, mom, plan = run(
        load_kernel,
        [ANY] * 3,
        [near, moment, table],
        scratch=[pltpu.SMEM((mats,), jnp.int32), pltpu.SemaphoreType.DMA((3,))],
        moved=2**21,
    )(far(grads), far(momentum), far(owner_slot))
    mom_other, plan, grads = lax.optimization_barrier((mom_other, plan, grads))
    grads_other = swap_cores(grads)
    (mom_out,) = run(give_kernel, [VMEM] * 3, [moment], moved=2**18)(plan, mom, mom_other)
    mom_x = across(mom_out, 1, 1, 0)
    mom_y = across(mom_out, 1, 0, 1)
    to_d, to_x, to_y = run(sum_kernel, [VMEM] * 3, [piece, piece, piece], moved=2**20)(
        plan, own, grads_other
    )
    in_d = across(to_d, 1, 1, 1)
    in_x = across(to_x, 1, 1, 0)
    in_y = across(to_y, 1, 0, 1)
    new, current = run(nesterov_kernel, [VMEM] * 10, [moment, whole], moved=2**20)(
        plan, mom_other, mom_x, mom_y, grads_other, in_d, in_x, in_y, own, mom
    )
    new_x = across(new, 0, 1, 0)
    new_y = across(new, 0, 0, 1)
    new_l = swap_cores(new)
    others, mine = run(orthogonalize_kernel, [VMEM], [update, update], moved=2**20)(current)
    up_x = across(mine, 0, 1, 0)
    up_y = across(others, 0, 0, 1)
    up_d = across(others, 0, 1, 1)
    up_l = swap_cores(mine)
    back, hold = run(back_kernel, [VMEM] * 5, [moment, moment], moved=2**19)(
        plan, mom, new_x, new_y, new_l
    )
    back_in = swap_cores(back)
    over_x, over_y, over_d = swap_cores(up_x), swap_cores(up_y), swap_cores(up_d)
    updates, new_momentum = run(
        finish_kernel,
        [VMEM] * 12,
        [jax.ShapeDtypeStruct((mats, half, width), bf16), jax.ShapeDtypeStruct(momentum.shape, bf16)],
        out_specs=[ANY, ANY],
        scratch=[pltpu.SemaphoreType.DMA((5,))],
        moved=2**20,
    )(plan, new, back_in, hold, up_x, up_y, up_d, up_l, over_x, over_y, over_d, mine)
    return (updates, new_momentum)


def solution(mesh):
    placed = (P("dp", "expert", "fsdp", None), P("expert"), P(("dp", "expert", "fsdp"), None, None))
    n_replica, n_shard = mesh.shape["dp"], mesh.shape["fsdp"]

    def per_device(grads, owner_slot, momentum):
        mats, cap = grads.shape[1], momentum.shape[0]
        if (n_replica, n_shard, mats, cap) == (4, 2, 4, 1):
            return per_device_chips(grads, owner_slot, momentum)
        return per_device_general(grads, owner_slot, momentum)

    return jax.shard_map(
        per_device,
        mesh=mesh,
        in_specs=placed,
        out_specs=(P("expert", "fsdp", None), P(("dp", "expert", "fsdp"), None, None)),
        check_vma=False,
    )
```

```python
import functools
import math

import jax
import jax.numpy as jnp
from jax import lax
from jax.experimental import pallas as pl
from jax.experimental.pallas import tpu as pltpu
from jax.sharding import PartitionSpec as P

R = 256
C = 512
ITERS = 5


COEF_A = 3.4445
COEF_B = -4.775
COEF_C = 2.0315
MOMENT = 0.95
FACTOR = 0.2 * math.sqrt(max(R, C))

AXES = ("dp", "fsdp")
VMEM = pl.BlockSpec(memory_space=pltpu.VMEM)
ANY = pl.BlockSpec(memory_space=pl.ANY)


def orthogonalize(stack):
    norms = jnp.sqrt(jnp.sum(stack * stack, axis=(1, 2), keepdims=True))
    current = stack / (norms + 1e-07)
    for step in range(ITERS):
        gram = jnp.einsum("krc,ksc->krs", current, current, precision=lax.Precision.HIGHEST)
        square = jnp.einsum("krs,kst->krt", gram, gram, precision=lax.Precision.HIGHEST)
        poly = COEF_B * gram + COEF_C * square
        current = COEF_A * current + jnp.einsum(
            "krs,ksc->krc", poly, current, precision=lax.Precision.HIGHEST
        )
    return current


def per_device_general(grads, owner_slot, momentum):
    partial_rows = grads[0]
    mats, rows_shard, width = partial_rows.shape
    n_replica = lax.axis_size("dp")
    n_shard = lax.axis_size("fsdp")
    owners = n_replica * n_shard
    cap = momentum.shape[0]
    rows_owner = rows_shard // n_replica
    reduced = lax.psum_scatter(partial_rows, "dp", scatter_dimension=1, tiled=True)
    slot_ids = jnp.arange(owners * cap, dtype=jnp.int32)
    matched = owner_slot[None, :] == slot_ids[:, None]
    holder = jnp.sum(jnp.where(matched, jnp.arange(mats, dtype=jnp.int32)[None, :], 0), axis=1)
    filled = jnp.any(matched, axis=1)
    outgoing = jnp.where(filled[:, None, None], jnp.take(reduced, holder, axis=0), 0.0)
    arrived = lax.all_to_all(
        outgoing.reshape(owners, cap, rows_owner, width),
        ("dp", "fsdp"),
        split_axis=0,
        concat_axis=0,
        tiled=True,
    )
    arrived = arrived.reshape(n_replica, n_shard, cap, rows_owner, width)
    whole = jnp.transpose(arrived, (2, 1, 0, 3, 4)).reshape(
        cap, n_shard * n_replica * rows_owner, width
    )
    buffer = MOMENT * momentum.astype(jnp.float32) + whole
    new_momentum = buffer.astype(jnp.bfloat16)
    nesterov = whole + MOMENT * buffer
    ortho = (FACTOR * orthogonalize(nesterov)).astype(jnp.bfloat16)
    leaving = jnp.transpose(
        ortho.reshape(cap, n_shard, n_replica, rows_owner, width), (2, 1, 0, 3, 4)
    )
    returned = lax.all_to_all(
        leaving.reshape(owners, cap, rows_owner, width),
        ("dp", "fsdp"),
        split_axis=0,
        concat_axis=0,
        tiled=True,
    )
    returned = returned.reshape(owners * cap, rows_owner, width)
    mine = jnp.take(returned, owner_slot, axis=0)
    updates = lax.all_gather(mine, "dp", axis=1, tiled=True)
    return (updates, new_momentum)


def here():
    d = lax.axis_index("dp")
    return d // 2, d % 2, lax.axis_index("fsdp")


def matrix_at(slots, chip, core):
    slot = (chip // 2) * 4 + core * 2 + chip % 2
    found = jnp.int32(-1)
    for j in range(4):
        found = jnp.where(slots[j] == slot, jnp.int32(j), found)
    return found


def deal(slots):
    at = [[matrix_at(slots, chip, core) for core in (0, 1)] for chip in range(4)]
    one, zero = jnp.int32(1), jnp.int32(0)
    extra = [
        jnp.where(at[q][0] >= 0, one, zero) + jnp.where(at[q][1] >= 0, one, zero) - 1
        for q in range(4)
    ]
    row = [extra[y] + extra[2 + y] for y in (0, 1)]
    out_y = [
        jnp.where((row[q % 2] > 0) & (extra[q ^ 1] < 0), one, zero) for q in range(4)
    ]
    out_x = [
        jnp.where(extra[q] - out_y[q] + out_y[q ^ 1] > 0, one, zero) for q in range(4)
    ]
    keep = [jnp.where(at[q][0] >= 0, at[q][0], at[q][1]) for q in range(4)]
    give = [jnp.where(at[q][1] >= 0, at[q][1], at[q][0]) for q in range(4)]
    matrix = [
        jnp.clip(
            jnp.where(
                out_y[q ^ 1] > 0, give[q ^ 1], jnp.where(out_x[q ^ 2] > 0, give[q ^ 2], keep[q])
            ),
            0,
            3,
        )
        for q in range(4)
    ]
    return at, out_x, out_y, matrix


def pick(values, index):
    result = values[0]
    for k in range(1, len(values)):
        result = jnp.where(index == k, values[k], result)
    return result


def load_kernel(
    grads, momentum, slots, grads_near, momentum_near, faded, plan, slots_near, sems
):
    copies = [
        pltpu.make_async_copy(source, target, sems.at[k])
        for k, (source, target) in enumerate(
            ((slots, slots_near), (momentum.at[0], momentum_near), (grads.at[0], grads_near))
        )
    ]
    for copy in copies:
        copy.start()
    copies[0].wait()
    x, c, y = here()
    at, out_x, out_y, matrix = deal([slots_near[j] for j in range(4)])
    q = 2 * x + y
    one, zero = jnp.int32(1), jnp.int32(0)
    at_0 = pick([at[k][0] for k in range(4)], q) >= 0
    at_1 = pick([at[k][1] for k in range(4)], q) >= 0
    leaves_x = pick(out_x, q)
    leaves_y = pick(out_y, q)
    comes_x = pick([out_x[k ^ 2] for k in range(4)], q) > 0
    comes_y = pick([out_y[k ^ 1] for k in range(4)], q) > 0
    mine = jnp.where(c == 0, at_0, at_1)
    away = jnp.where((c == 1) | jnp.logical_not(at_1), leaves_x + 2 * leaves_y, zero)
    entries = [pick([matrix[k ^ flip] for k in range(4)], q) for flip in range(4)]
    entries.append(jnp.where(comes_y, 3, jnp.where(comes_x, 2, jnp.where(at_0, zero, one))))
    entries.append(jnp.where(at_1, one, zero))
    entries.append(jnp.where(mine, one + away, zero))
    row = lax.broadcasted_iota(jnp.int32, plan.shape, 0)
    table = jnp.zeros(plan.shape, jnp.int32)
    for k, entry in enumerate(entries):
        table = jnp.where(row == k, entry, table)
    plan[...] = table
    copies[1].wait()
    faded[...] = (MOMENT * momentum_near[...].astype(jnp.float32)).astype(jnp.bfloat16)
    copies[2].wait()


SOURCE, GIVER, SLOT = 4, 5, 6


def give_kernel(plan, mom, mom_other, mom_out):
    _, c, _ = here()

    @pl.when(c == 1)
    def _():
        mine = plan[GIVER, 0] == 1
        mom_out[...] = jnp.where(mine, mom[...], mom_other[0])


def sum_kernel(plan, own, other, to_d, to_x, to_y):
    _, c, _ = here()

    @pl.when(c == 1)
    def _():
        for out, flip in ((to_d, 3), (to_x, 2), (to_y, 1)):
            m = plan[flip, 0]
            out[...] = own[m] + other[0, m]


def parts_of(value):
    high = value.astype(jnp.bfloat16)
    return high, (value - high.astype(jnp.float32)).astype(jnp.bfloat16)


def polynomial_step(current):
    dot = functools.partial(lax.dot_general, preferred_element_type=jnp.float32)
    plain, turned = (((1,), (0,)), ((), ())), (((1,), (1,)), ((), ()))
    high, low = parts_of(current)
    mixed = dot(high, low, turned)
    gram = dot(high, high, turned) + (mixed + mixed.T)
    gram_high, gram_low = parts_of(gram)
    rows = current.shape[0] // 2
    blocks = []
    for k in (0, 1):
        block = slice(k * rows, (k + 1) * rows)
        square = dot(gram_high[block], gram_high, plain) + (
            dot(gram_high[block], gram_low, plain) + dot(gram_low[block], gram_high, plain)
        )
        poly_high, poly_low = parts_of(COEF_B * gram[block] + COEF_C * square)
        change = dot(poly_high, high, plain) + (
            dot(poly_high, low, plain) + dot(poly_low, high, plain)
        )
        blocks.append(COEF_A * current[block] + change)
    return jnp.concatenate(blocks, axis=0)


def nesterov_kernel(
    plan, mom_other, mom_x, mom_y, other, in_d, in_x, in_y, own, mom, new, current
):
    _, c, y = here()
    half = own.shape[1]

    @pl.when(c == 0)
    def _():
        m = plan[0, 0]
        source = plan[SOURCE, 0]
        squares = jnp.float32(0)
        pieces = []
        for part, start in enumerate((y * half, (1 - y) * half)):
            rows = pl.ds(pl.multiple_of(start, half), half)
            if part == 0:
                total = (own[m] + other[0, m]) + in_x[...]
            else:
                total = in_y[...] + in_d[...]
            held = pick([mom[rows], mom_other[0, rows], mom_x[rows], mom_y[rows]], source)
            buffer = MOMENT * held.astype(jnp.float32) + total
            new[rows] = buffer.astype(jnp.bfloat16)
            piece = total + MOMENT * buffer
            squares = squares + jnp.sum(piece * piece)
            pieces.append(piece)
        norm = jnp.sqrt(squares) + 1e-07
        for part in (0, 1):
            current[part * half : (part + 1) * half] = pieces[part] / norm


def middle_kernel(steps, before, after):
    _, c, _ = here()

    @pl.when(c == 0)
    def _():
        value = before[...]
        for _ in range(steps):
            value = polynomial_step(value)
        after[...] = value


def last_kernel(steps, start, others, mine):
    _, c, _ = here()
    half = mine.shape[0]

    @pl.when(c == 0)
    def _():
        value = start[...]
        for _ in range(steps):
            value = polynomial_step(value)
        value = (FACTOR * value).astype(jnp.bfloat16)
        mine[...] = value[:half]
        others[...] = value[half:]


def finish_kernel(
    plan, faded, new, back, back_in, up_d, up_x, up_y, up_l, in_d, in_x, in_y, mine,
    updates, moment, sems,
):
    _, c, _ = here()
    for core, sources in ((0, (mine, in_y, in_x, in_d)), (1, (up_l, up_y, up_x, up_d))):

        @pl.when(c == core)
        def _():
            for flip, source in enumerate(sources):
                m = plan[flip, 0]
                pltpu.make_async_copy(source, updates.at[m], sems.at[flip]).start()

    slot = plan[SLOT, 0]
    handed = (slot == 3) & (c == 1)
    for chosen, source in (
        (slot == 0, faded),
        (slot == 1, new),
        ((slot > 1) & jnp.logical_not(handed), back),
        (handed, back_in),
    ):

        @pl.when(chosen)
        def _():
            pltpu.make_async_copy(source, moment.at[0], sems.at[4]).start()

    for flip in range(4):
        pltpu.make_async_copy(mine, updates.at[flip], sems.at[flip]).wait()
    pltpu.make_async_copy(faded, moment.at[0], sems.at[4]).wait()


def chip_device(x, c, y):
    return (2 * x + c) * 2 + y


CHIPS = [(x, y) for x in (0, 1) for y in (0, 1)]


def swap_cores(value):
    pairs = [
        (chip_device(x, c, y), chip_device(x, 1 - c, y)) for x, y in CHIPS for c in (0, 1)
    ]
    return lax.ppermute(value, AXES, pairs)


def across(value, sender, flip_x, flip_y):
    pairs = [
        (chip_device(x, sender, y), chip_device(x ^ flip_x, 1 - sender, y ^ flip_y))
        for x, y in CHIPS
    ]
    pairs += [(chip_device(x, 1 - sender, y), chip_device(x, sender, y)) for x, y in CHIPS]
    return lax.ppermute(value, AXES, pairs)


def both_ways(value):
    pairs = [(chip_device(x, 0, y), chip_device(1 - x, 1, y)) for x, y in CHIPS]
    pairs += [(chip_device(x, 1, y), chip_device(x, 0, 1 - y)) for x, y in CHIPS]
    return lax.ppermute(value, AXES, pairs)


def run(kernel, in_specs, out_shapes, out_specs=None, scratch=(), flops=0, moved=0):
    return pl.pallas_call(
        kernel,
        in_specs=in_specs,
        out_shape=out_shapes,
        out_specs=out_specs if out_specs is not None else [VMEM] * len(out_shapes),
        scratch_shapes=list(scratch),
        compiler_params=pltpu.CompilerParams(vmem_limit_bytes=24 * 2**20),
        cost_estimate=pl.CostEstimate(flops=flops, bytes_accessed=moved, transcendentals=0),
    )


def per_device_chips(grads, owner_slot, momentum):
    _, mats, half, width = grads.shape
    rows = momentum.shape[1]
    f32, bf16 = jnp.float32, jnp.bfloat16
    piece = jax.ShapeDtypeStruct((half, width), f32)
    whole = jax.ShapeDtypeStruct((rows, width), f32)
    moment = jax.ShapeDtypeStruct((rows, width), bf16)
    update = jax.ShapeDtypeStruct((half, width), bf16)

    near = jax.ShapeDtypeStruct((mats, half, width), f32)
    table = jax.ShapeDtypeStruct((8, 128), jnp.int32)

    mom_other = swap_cores(momentum)
    far = functools.partial(pltpu.with_memory_space_constraint, memory_space=pltpu.HBM)
    own, mom, faded, plan = run(
        load_kernel,
        [ANY] * 3,
        [near, moment, moment, table],
        scratch=[pltpu.SMEM((mats,), jnp.int32), pltpu.SemaphoreType.DMA((3,))],
        moved=2**21,
    )(far(grads), far(momentum), far(owner_slot))
    mom_other, plan, grads = lax.optimization_barrier((mom_other, plan, grads))
    grads_other = swap_cores(grads)
    (mom_out,) = run(give_kernel, [VMEM] * 3, [moment], moved=2**18)(plan, mom, mom_other)
    mom_x = across(mom_out, 1, 1, 0)
    mom_y = across(mom_out, 1, 0, 1)
    to_d, to_x, to_y = run(sum_kernel, [VMEM] * 3, [piece, piece, piece], moved=2**20)(
        plan, own, grads_other
    )
    in_d = across(to_d, 1, 1, 1)
    in_x = across(to_x, 1, 1, 0)
    in_y = across(to_y, 1, 0, 1)
    new, current = run(nesterov_kernel, [VMEM] * 10, [moment, whole], moved=2**20)(
        plan, mom_other, mom_x, mom_y, grads_other, in_d, in_x, in_y, own, mom
    )
    new_l = swap_cores(new)
    (current,) = run(functools.partial(middle_kernel, 2), [VMEM], [whole], moved=2**20)(current)
    new_l, current = lax.optimization_barrier((new_l, current))
    new = jnp.where(lax.axis_index("dp") % 2 == 0, new, new_l)
    back = both_ways(new)
    others, mine = run(
        functools.partial(last_kernel, ITERS - 2), [VMEM], [update, update], moved=2**20
    )(current)
    up_d = across(others, 0, 1, 1)
    up_x = across(mine, 0, 1, 0)
    up_y = across(others, 0, 0, 1)
    up_l = swap_cores(mine)
    back_in = swap_cores(back)
    over_d, over_x, over_y = swap_cores(up_d), swap_cores(up_x), swap_cores(up_y)
    updates, new_momentum = run(
        finish_kernel,
        [VMEM] * 13,
        [jax.ShapeDtypeStruct((mats, half, width), bf16), jax.ShapeDtypeStruct(momentum.shape, bf16)],
        out_specs=[ANY, ANY],
        scratch=[pltpu.SemaphoreType.DMA((5,))],
        moved=2**20,
    )(plan, faded, new, back, back_in, up_d, up_x, up_y, up_l, over_d, over_x, over_y, mine)
    return (updates, new_momentum)


def solution(mesh):
    placed = (P("dp", "expert", "fsdp", None), P("expert"), P(("dp", "expert", "fsdp"), None, None))
    n_replica, n_shard = mesh.shape["dp"], mesh.shape["fsdp"]

    def per_device(grads, owner_slot, momentum):
        mats, cap = grads.shape[1], momentum.shape[0]
        if (n_replica, n_shard, mats, cap) == (4, 2, 4, 1):
            return per_device_chips(grads, owner_slot, momentum)
        return per_device_general(grads, owner_slot, momentum)

    return jax.shard_map(
        per_device,
        mesh=mesh,
        in_specs=placed,
        out_specs=(P("expert", "fsdp", None), P(("dp", "expert", "fsdp"), None, None)),
        check_vma=False,
    )
```

```python
import functools
import math

import jax
import jax.numpy as jnp
from jax import lax
from jax.experimental import pallas as pl
from jax.experimental.pallas import tpu as pltpu
from jax.sharding import PartitionSpec as P

R = 256
C = 512
ITERS = 5


COEF_A = 3.4445
COEF_B = -4.775
COEF_C = 2.0315
MOMENT = 0.95
FACTOR = 0.2 * math.sqrt(max(R, C))

AXES = ("dp", "fsdp")
VMEM = pl.BlockSpec(memory_space=pltpu.VMEM)
ANY = pl.BlockSpec(memory_space=pl.ANY)


def orthogonalize(stack):
    norms = jnp.sqrt(jnp.sum(stack * stack, axis=(1, 2), keepdims=True))
    current = stack / (norms + 1e-07)
    for step in range(ITERS):
        gram = jnp.einsum("krc,ksc->krs", current, current, precision=lax.Precision.HIGHEST)
        square = jnp.einsum("krs,kst->krt", gram, gram, precision=lax.Precision.HIGHEST)
        poly = COEF_B * gram + COEF_C * square
        current = COEF_A * current + jnp.einsum(
            "krs,ksc->krc", poly, current, precision=lax.Precision.HIGHEST
        )
    return current


def per_device_general(grads, owner_slot, momentum):
    partial_rows = grads[0]
    mats, rows_shard, width = partial_rows.shape
    n_replica = lax.axis_size("dp")
    n_shard = lax.axis_size("fsdp")
    owners = n_replica * n_shard
    cap = momentum.shape[0]
    rows_owner = rows_shard // n_replica
    reduced = lax.psum_scatter(partial_rows, "dp", scatter_dimension=1, tiled=True)
    slot_ids = jnp.arange(owners * cap, dtype=jnp.int32)
    matched = owner_slot[None, :] == slot_ids[:, None]
    holder = jnp.sum(jnp.where(matched, jnp.arange(mats, dtype=jnp.int32)[None, :], 0), axis=1)
    filled = jnp.any(matched, axis=1)
    outgoing = jnp.where(filled[:, None, None], jnp.take(reduced, holder, axis=0), 0.0)
    arrived = lax.all_to_all(
        outgoing.reshape(owners, cap, rows_owner, width),
        ("dp", "fsdp"),
        split_axis=0,
        concat_axis=0,
        tiled=True,
    )
    arrived = arrived.reshape(n_replica, n_shard, cap, rows_owner, width)
    whole = jnp.transpose(arrived, (2, 1, 0, 3, 4)).reshape(
        cap, n_shard * n_replica * rows_owner, width
    )
    buffer = MOMENT * momentum.astype(jnp.float32) + whole
    new_momentum = buffer.astype(jnp.bfloat16)
    nesterov = whole + MOMENT * buffer
    ortho = (FACTOR * orthogonalize(nesterov)).astype(jnp.bfloat16)
    leaving = jnp.transpose(
        ortho.reshape(cap, n_shard, n_replica, rows_owner, width), (2, 1, 0, 3, 4)
    )
    returned = lax.all_to_all(
        leaving.reshape(owners, cap, rows_owner, width),
        ("dp", "fsdp"),
        split_axis=0,
        concat_axis=0,
        tiled=True,
    )
    returned = returned.reshape(owners * cap, rows_owner, width)
    mine = jnp.take(returned, owner_slot, axis=0)
    updates = lax.all_gather(mine, "dp", axis=1, tiled=True)
    return (updates, new_momentum)


def here():
    d = lax.axis_index("dp")
    return d // 2, d % 2, lax.axis_index("fsdp")


def matrix_at(slots, chip, core):
    slot = (chip // 2) * 4 + core * 2 + chip % 2
    found = jnp.int32(-1)
    for j in range(4):
        found = jnp.where(slots[j] == slot, jnp.int32(j), found)
    return found


def deal(slots):
    at = [[matrix_at(slots, chip, core) for core in (0, 1)] for chip in range(4)]
    one, zero = jnp.int32(1), jnp.int32(0)
    extra = [
        jnp.where(at[q][0] >= 0, one, zero) + jnp.where(at[q][1] >= 0, one, zero) - 1
        for q in range(4)
    ]
    row = [extra[y] + extra[2 + y] for y in (0, 1)]
    out_y = [
        jnp.where((row[q % 2] > 0) & (extra[q ^ 1] < 0), one, zero) for q in range(4)
    ]
    out_x = [
        jnp.where(extra[q] - out_y[q] + out_y[q ^ 1] > 0, one, zero) for q in range(4)
    ]
    keep = [jnp.where(at[q][0] >= 0, at[q][0], at[q][1]) for q in range(4)]
    give = [jnp.where(at[q][1] >= 0, at[q][1], at[q][0]) for q in range(4)]
    matrix = [
        jnp.clip(
            jnp.where(
                out_y[q ^ 1] > 0, give[q ^ 1], jnp.where(out_x[q ^ 2] > 0, give[q ^ 2], keep[q])
            ),
            0,
            3,
        )
        for q in range(4)
    ]
    return at, out_x, out_y, matrix


def pick(values, index):
    result = values[0]
    for k in range(1, len(values)):
        result = jnp.where(index == k, values[k], result)
    return result


def load_kernel(
    grads, momentum, slots, grads_near, momentum_near, faded, plan, slots_near, sems
):
    copies = [
        pltpu.make_async_copy(source, target, sems.at[k])
        for k, (source, target) in enumerate(
            ((slots, slots_near), (momentum.at[0], momentum_near), (grads.at[0], grads_near))
        )
    ]
    for copy in copies:
        copy.start()
    copies[0].wait()
    x, c, y = here()
    at, out_x, out_y, matrix = deal([slots_near[j] for j in range(4)])
    q = 2 * x + y
    one, zero = jnp.int32(1), jnp.int32(0)
    at_0 = pick([at[k][0] for k in range(4)], q) >= 0
    at_1 = pick([at[k][1] for k in range(4)], q) >= 0
    leaves_x = pick(out_x, q)
    leaves_y = pick(out_y, q)
    comes_x = pick([out_x[k ^ 2] for k in range(4)], q) > 0
    comes_y = pick([out_y[k ^ 1] for k in range(4)], q) > 0
    mine = jnp.where(c == 0, at_0, at_1)
    away = jnp.where((c == 1) | jnp.logical_not(at_1), leaves_x + 2 * leaves_y, zero)
    entries = [pick([matrix[k ^ flip] for k in range(4)], q) for flip in range(4)]
    entries.append(jnp.where(comes_y, 3, jnp.where(comes_x, 2, jnp.where(at_0, zero, one))))
    entries.append(jnp.where(at_1, one, zero))
    entries.append(jnp.where(mine, one + away, zero))
    row = lax.broadcasted_iota(jnp.int32, plan.shape, 0)
    table = jnp.zeros(plan.shape, jnp.int32)
    for k, entry in enumerate(entries):
        table = jnp.where(row == k, entry, table)
    plan[...] = table
    copies[1].wait()
    faded[...] = (MOMENT * momentum_near[...].astype(jnp.float32)).astype(jnp.bfloat16)
    copies[2].wait()


SOURCE, GIVER, SLOT = 4, 5, 6


def give_kernel(plan, mom, mom_other, mom_out):
    _, c, _ = here()

    @pl.when(c == 1)
    def _():
        mine = plan[GIVER, 0] == 1
        mom_out[...] = jnp.where(mine, mom[...], mom_other[0])


def sum_kernel(plan, own, other, to_d, to_x, to_y):
    _, c, _ = here()

    @pl.when(c == 1)
    def _():
        for out, flip in ((to_d, 3), (to_x, 2), (to_y, 1)):
            m = plan[flip, 0]
            out[...] = own[m] + other[0, m]


def parts_of(value):
    high = value.astype(jnp.bfloat16)
    return high, (value - high.astype(jnp.float32)).astype(jnp.bfloat16)


def polynomial_step(current):
    dot = functools.partial(lax.dot_general, preferred_element_type=jnp.float32)
    plain, turned = (((1,), (0,)), ((), ())), (((1,), (1,)), ((), ()))
    high, low = parts_of(current)
    mixed = dot(high, low, turned).astype(jnp.bfloat16)
    gram = dot(high, high, turned) + (mixed.astype(jnp.float32) + mixed.T.astype(jnp.float32))
    gram_high, gram_low = parts_of(gram)
    rows = current.shape[0] // 2
    blocks = []
    for k in (0, 1):
        block = slice(k * rows, (k + 1) * rows)
        square = dot(gram_high[block], gram_high, plain) + (
            dot(gram_high[block], gram_low, plain) + dot(gram_low[block], gram_high, plain)
        )
        poly_high, poly_low = parts_of(COEF_B * gram[block] + COEF_C * square)
        change = dot(poly_high, high, plain) + (
            dot(poly_high, low, plain) + dot(poly_low, high, plain)
        )
        blocks.append(COEF_A * current[block] + change)
    return jnp.concatenate(blocks, axis=0)


def ready_kernel(plan, mom_other, mom_x, mom_y, other, own, mom, base, held):
    _, c, y = here()
    half = own.shape[1]

    @pl.when(c == 0)
    def _():
        m = plan[0, 0]
        source = plan[SOURCE, 0]
        base[...] = own[m] + other[0, m]
        for part, start in enumerate((y * half, (1 - y) * half)):
            rows = pl.ds(pl.multiple_of(start, half), half)
            held[part * half : (part + 1) * half] = pick(
                [mom[rows], mom_other[0, rows], mom_x[rows], mom_y[rows]], source
            )


def nesterov_kernel(base, held, in_d, in_x, in_y, new, nesterov, scale):
    _, c, y = here()
    half = base.shape[0]

    @pl.when(c == 0)
    def _():
        squares = jnp.zeros((1, base.shape[1]), jnp.float32)
        for part, start in enumerate((y * half, (1 - y) * half)):
            rows = pl.ds(pl.multiple_of(start, half), half)
            local = slice(part * half, (part + 1) * half)
            total = base[...] + in_x[...] if part == 0 else in_y[...] + in_d[...]
            buffer = MOMENT * held[local].astype(jnp.float32) + total
            new[rows] = buffer.astype(jnp.bfloat16)
            piece = total + MOMENT * buffer
            nesterov[local] = piece
            squares = squares + jnp.sum(piece * piece, axis=0, keepdims=True)
        norm = jnp.sqrt(jnp.sum(squares, axis=1, keepdims=True)) + 1e-07
        scale[...] = jnp.broadcast_to(1.0 / norm, scale.shape)


def middle_kernel(steps, scale, before, after):
    _, c, _ = here()

    @pl.when(c == 0)
    def _():
        value = before[...] * scale[0:1, 0:1]
        for _ in range(steps):
            value = polynomial_step(value)
        after[...] = value


def last_kernel(steps, start, others, mine):
    _, c, _ = here()
    half = mine.shape[0]

    @pl.when(c == 0)
    def _():
        value = start[...]
        for _ in range(steps):
            value = polynomial_step(value)
        value = (FACTOR * value).astype(jnp.bfloat16)
        mine[...] = value[:half]
        others[...] = value[half:]


def place(plan, core, pieces, updates, sems):
    _, c, _ = here()

    @pl.when(c == core)
    def _():
        for k, (flip, source) in enumerate(pieces):
            pltpu.make_async_copy(source, updates.at[plan[flip, 0]], sems.at[k]).start()


def early_kernel(plan, up_d, up_l, in_d, mine, updates, sems):
    place(plan, 0, ((0, mine), (3, in_d)), updates, sems)
    place(plan, 1, ((0, up_l), (3, up_d)), updates, sems)
    for k in (0, 1):
        pltpu.make_async_copy(mine, updates.at[k], sems.at[k]).wait()


def finish_kernel(
    plan, faded, new, back, back_in, up_x, up_y, in_x, in_y, _, updates, moment, sems
):
    _, c, _ = here()
    place(plan, 0, ((2, in_x), (1, in_y)), updates, sems)
    place(plan, 1, ((2, up_x), (1, up_y)), updates, sems)
    slot = plan[SLOT, 0]
    handed = (slot == 3) & (c == 1)
    for chosen, source in (
        (slot == 0, faded),
        (slot == 1, new),
        ((slot > 1) & jnp.logical_not(handed), back),
        (handed, back_in),
    ):

        @pl.when(chosen)
        def _():
            pltpu.make_async_copy(source, moment.at[0], sems.at[2]).start()

    for k in (0, 1):
        pltpu.make_async_copy(up_x, updates.at[k], sems.at[k]).wait()
    pltpu.make_async_copy(faded, moment.at[0], sems.at[2]).wait()


def chip_device(x, c, y):
    return (2 * x + c) * 2 + y


CHIPS = [(x, y) for x in (0, 1) for y in (0, 1)]


def swap_cores(value):
    pairs = [
        (chip_device(x, c, y), chip_device(x, 1 - c, y)) for x, y in CHIPS for c in (0, 1)
    ]
    return lax.ppermute(value, AXES, pairs)


def across(value, sender, flip_x, flip_y):
    pairs = [
        (chip_device(x, sender, y), chip_device(x ^ flip_x, 1 - sender, y ^ flip_y))
        for x, y in CHIPS
    ]
    pairs += [(chip_device(x, 1 - sender, y), chip_device(x, sender, y)) for x, y in CHIPS]
    return lax.ppermute(value, AXES, pairs)


def both_ways(value):
    pairs = [(chip_device(x, 0, y), chip_device(1 - x, 1, y)) for x, y in CHIPS]
    pairs += [(chip_device(x, 1, y), chip_device(x, 0, 1 - y)) for x, y in CHIPS]
    return lax.ppermute(value, AXES, pairs)


def run(kernel, in_specs, out_shapes, out_specs=None, scratch=(), moved=0, aliases={}):
    return pl.pallas_call(
        kernel,
        in_specs=in_specs,
        out_shape=out_shapes,
        out_specs=out_specs if out_specs is not None else [VMEM] * len(out_shapes),
        scratch_shapes=list(scratch),
        input_output_aliases=aliases,
        compiler_params=pltpu.CompilerParams(vmem_limit_bytes=24 * 2**20),
        cost_estimate=pl.CostEstimate(flops=0, bytes_accessed=moved, transcendentals=0),
    )


def per_device_chips(grads, owner_slot, momentum):
    _, mats, half, width = grads.shape
    rows = momentum.shape[1]
    f32, bf16 = jnp.float32, jnp.bfloat16
    piece = jax.ShapeDtypeStruct((half, width), f32)
    whole = jax.ShapeDtypeStruct((rows, width), f32)
    moment = jax.ShapeDtypeStruct((rows, width), bf16)
    update = jax.ShapeDtypeStruct((half, width), bf16)

    near = jax.ShapeDtypeStruct((mats, half, width), f32)
    table = jax.ShapeDtypeStruct((8, 128), jnp.int32)

    mom_other = swap_cores(momentum)
    far = functools.partial(pltpu.with_memory_space_constraint, memory_space=pltpu.HBM)
    own, mom, faded, plan = run(
        load_kernel,
        [ANY] * 3,
        [near, moment, moment, table],
        scratch=[pltpu.SMEM((mats,), jnp.int32), pltpu.SemaphoreType.DMA((3,))],
        moved=2**21,
    )(far(grads), far(momentum), far(owner_slot))
    mom_other, plan, grads = lax.optimization_barrier((mom_other, plan, grads))
    grads_other = swap_cores(grads)
    (mom_out,) = run(give_kernel, [VMEM] * 3, [moment], moved=2**18)(plan, mom, mom_other)
    mom_x = across(mom_out, 1, 1, 0)
    mom_y = across(mom_out, 1, 0, 1)
    to_d, to_x, to_y = run(sum_kernel, [VMEM] * 3, [piece, piece, piece], moved=2**20)(
        plan, own, grads_other
    )
    in_d = across(to_d, 1, 1, 1)
    in_x = across(to_x, 1, 1, 0)
    in_y = across(to_y, 1, 0, 1)
    base, held = run(ready_kernel, [VMEM] * 7, [piece, moment], moved=2**20)(
        plan, mom_other, mom_x, mom_y, grads_other, own, mom
    )
    new, current, scale = run(
        nesterov_kernel,
        [VMEM] * 5,
        [moment, whole, jax.ShapeDtypeStruct((8, 128), f32)],
        moved=2**20,
    )(base, held, in_d, in_x, in_y)
    new_l = swap_cores(new)
    (current,) = run(functools.partial(middle_kernel, 2), [VMEM] * 2, [whole], moved=2**20)(
        scale, current
    )
    new_l, current = lax.optimization_barrier((new_l, current))
    new = jnp.where(lax.axis_index("dp") % 2 == 0, new, new_l)
    back = both_ways(new)
    others, mine = run(
        functools.partial(last_kernel, ITERS - 2), [VMEM], [update, update], moved=2**20
    )(current)
    up_d = across(others, 0, 1, 1)
    up_x = across(mine, 0, 1, 0)
    up_y = across(others, 0, 0, 1)
    up_l = swap_cores(mine)
    back_in = swap_cores(back)
    over_d, over_x, over_y = swap_cores(up_d), swap_cores(up_x), swap_cores(up_y)
    whole_updates = jax.ShapeDtypeStruct((mats, half, width), bf16)
    (updates,) = run(
        early_kernel,
        [VMEM] * 5,
        [whole_updates],
        out_specs=[ANY],
        scratch=[pltpu.SemaphoreType.DMA((2,))],
        moved=2**19,
    )(plan, up_d, up_l, over_d, mine)
    updates, new_momentum = run(
        finish_kernel,
        [VMEM] * 9 + [ANY],
        [whole_updates, jax.ShapeDtypeStruct(momentum.shape, bf16)],
        out_specs=[ANY, ANY],
        scratch=[pltpu.SemaphoreType.DMA((3,))],
        moved=2**20,
        aliases={9: 0},
    )(plan, faded, new, back, back_in, up_x, up_y, over_x, over_y, updates)
    return (updates, new_momentum)


def solution(mesh):
    placed = (P("dp", "expert", "fsdp", None), P("expert"), P(("dp", "expert", "fsdp"), None, None))
    n_replica, n_shard = mesh.shape["dp"], mesh.shape["fsdp"]

    def per_device(grads, owner_slot, momentum):
        mats, cap = grads.shape[1], momentum.shape[0]
        if (n_replica, n_shard, mats, cap) == (4, 2, 4, 1):
            return per_device_chips(grads, owner_slot, momentum)
        return per_device_general(grads, owner_slot, momentum)

    return jax.shard_map(
        per_device,
        mesh=mesh,
        in_specs=placed,
        out_specs=(P("expert", "fsdp", None), P(("dp", "expert", "fsdp"), None, None)),
        check_vma=False,
    )
```

```python
import functools
import math

import jax
import jax.numpy as jnp
from jax import lax
from jax.experimental import pallas as pl
from jax.experimental.pallas import tpu as pltpu
from jax.sharding import PartitionSpec as P

R = 256
C = 512
ITERS = 5


COEF_A = 3.4445
COEF_B = -4.775
COEF_C = 2.0315
MOMENT = 0.95
FACTOR = 0.2 * math.sqrt(max(R, C))

AXES = ("dp", "fsdp")
VMEM = pl.BlockSpec(memory_space=pltpu.VMEM)
ANY = pl.BlockSpec(memory_space=pl.ANY)


def orthogonalize(stack):
    norms = jnp.sqrt(jnp.sum(stack * stack, axis=(1, 2), keepdims=True))
    current = stack / (norms + 1e-07)
    for step in range(ITERS):
        gram = jnp.einsum("krc,ksc->krs", current, current, precision=lax.Precision.HIGHEST)
        square = jnp.einsum("krs,kst->krt", gram, gram, precision=lax.Precision.HIGHEST)
        poly = COEF_B * gram + COEF_C * square
        current = COEF_A * current + jnp.einsum(
            "krs,ksc->krc", poly, current, precision=lax.Precision.HIGHEST
        )
    return current


def per_device_general(grads, owner_slot, momentum):
    partial_rows = grads[0]
    mats, rows_shard, width = partial_rows.shape
    n_replica = lax.axis_size("dp")
    n_shard = lax.axis_size("fsdp")
    owners = n_replica * n_shard
    cap = momentum.shape[0]
    rows_owner = rows_shard // n_replica
    reduced = lax.psum_scatter(partial_rows, "dp", scatter_dimension=1, tiled=True)
    slot_ids = jnp.arange(owners * cap, dtype=jnp.int32)
    matched = owner_slot[None, :] == slot_ids[:, None]
    holder = jnp.sum(jnp.where(matched, jnp.arange(mats, dtype=jnp.int32)[None, :], 0), axis=1)
    filled = jnp.any(matched, axis=1)
    outgoing = jnp.where(filled[:, None, None], jnp.take(reduced, holder, axis=0), 0.0)
    arrived = lax.all_to_all(
        outgoing.reshape(owners, cap, rows_owner, width),
        ("dp", "fsdp"),
        split_axis=0,
        concat_axis=0,
        tiled=True,
    )
    arrived = arrived.reshape(n_replica, n_shard, cap, rows_owner, width)
    whole = jnp.transpose(arrived, (2, 1, 0, 3, 4)).reshape(
        cap, n_shard * n_replica * rows_owner, width
    )
    buffer = MOMENT * momentum.astype(jnp.float32) + whole
    new_momentum = buffer.astype(jnp.bfloat16)
    nesterov = whole + MOMENT * buffer
    ortho = (FACTOR * orthogonalize(nesterov)).astype(jnp.bfloat16)
    leaving = jnp.transpose(
        ortho.reshape(cap, n_shard, n_replica, rows_owner, width), (2, 1, 0, 3, 4)
    )
    returned = lax.all_to_all(
        leaving.reshape(owners, cap, rows_owner, width),
        ("dp", "fsdp"),
        split_axis=0,
        concat_axis=0,
        tiled=True,
    )
    returned = returned.reshape(owners * cap, rows_owner, width)
    mine = jnp.take(returned, owner_slot, axis=0)
    updates = lax.all_gather(mine, "dp", axis=1, tiled=True)
    return (updates, new_momentum)


def here():
    d = lax.axis_index("dp")
    return d // 2, d % 2, lax.axis_index("fsdp")


def matrix_at(slots, chip, core):
    slot = (chip // 2) * 4 + core * 2 + chip % 2
    found = jnp.int32(-1)
    for j in range(4):
        found = jnp.where(slots[j] == slot, jnp.int32(j), found)
    return found


def deal(slots):
    at = [[matrix_at(slots, chip, core) for core in (0, 1)] for chip in range(4)]
    one, zero = jnp.int32(1), jnp.int32(0)
    extra = [
        jnp.where(at[q][0] >= 0, one, zero) + jnp.where(at[q][1] >= 0, one, zero) - 1
        for q in range(4)
    ]
    row = [extra[y] + extra[2 + y] for y in (0, 1)]
    out_y = [
        jnp.where((row[q % 2] > 0) & (extra[q ^ 1] < 0), one, zero) for q in range(4)
    ]
    out_x = [
        jnp.where(extra[q] - out_y[q] + out_y[q ^ 1] > 0, one, zero) for q in range(4)
    ]
    keep = [jnp.where(at[q][0] >= 0, at[q][0], at[q][1]) for q in range(4)]
    give = [jnp.where(at[q][1] >= 0, at[q][1], at[q][0]) for q in range(4)]
    matrix = [
        jnp.clip(
            jnp.where(
                out_y[q ^ 1] > 0, give[q ^ 1], jnp.where(out_x[q ^ 2] > 0, give[q ^ 2], keep[q])
            ),
            0,
            3,
        )
        for q in range(4)
    ]
    return at, out_x, out_y, matrix


def pick(values, index):
    result = values[0]
    for k in range(1, len(values)):
        result = jnp.where(index == k, values[k], result)
    return result


def load_kernel(
    grads, momentum, slots, grads_near, momentum_near, faded, plan, slots_near, sems
):
    copies = [
        pltpu.make_async_copy(source, target, sems.at[k])
        for k, (source, target) in enumerate(
            ((slots, slots_near), (momentum.at[0], momentum_near), (grads.at[0], grads_near))
        )
    ]
    for copy in copies:
        copy.start()
    copies[0].wait()
    x, c, y = here()
    at, out_x, out_y, matrix = deal([slots_near[j] for j in range(4)])
    q = 2 * x + y
    one, zero = jnp.int32(1), jnp.int32(0)
    at_0 = pick([at[k][0] for k in range(4)], q) >= 0
    at_1 = pick([at[k][1] for k in range(4)], q) >= 0
    leaves_x = pick(out_x, q)
    leaves_y = pick(out_y, q)
    comes_x = pick([out_x[k ^ 2] for k in range(4)], q) > 0
    comes_y = pick([out_y[k ^ 1] for k in range(4)], q) > 0
    mine = jnp.where(c == 0, at_0, at_1)
    away = jnp.where((c == 1) | jnp.logical_not(at_1), leaves_x + 2 * leaves_y, zero)
    entries = [pick([matrix[k ^ flip] for k in range(4)], q) for flip in range(4)]
    entries.append(jnp.where(comes_y, 3, jnp.where(comes_x, 2, jnp.where(at_0, zero, one))))
    entries.append(jnp.where(at_1, one, zero))
    entries.append(jnp.where(mine, one + away, zero))
    row = lax.broadcasted_iota(jnp.int32, plan.shape, 0)
    table = jnp.zeros(plan.shape, jnp.int32)
    for k, entry in enumerate(entries):
        table = jnp.where(row == k, entry, table)
    plan[...] = table
    copies[1].wait()
    faded[...] = (MOMENT * momentum_near[...].astype(jnp.float32)).astype(jnp.bfloat16)
    copies[2].wait()


SOURCE, GIVER, SLOT = 4, 5, 6


def give_kernel(plan, mom, mom_other, mom_out):
    _, c, _ = here()

    @pl.when(c == 1)
    def _():
        mine = plan[GIVER, 0] == 1
        mom_out[...] = jnp.where(mine, mom[...], mom_other[0])


def sum_kernel(plan, own, other, to_d, to_x, to_y):
    _, c, _ = here()

    @pl.when(c == 1)
    def _():
        for out, flip in ((to_d, 3), (to_x, 2), (to_y, 1)):
            m = plan[flip, 0]
            out[...] = own[m] + other[0, m]


def parts_of(value):
    high = value.astype(jnp.bfloat16)
    return high, (value - high.astype(jnp.float32)).astype(jnp.bfloat16)


def gram_of(high, low):
    dot = functools.partial(lax.dot_general, preferred_element_type=jnp.float32)
    turned = (((1,), (1,)), ((), ()))
    mixed = dot(high, low, turned).astype(jnp.bfloat16)
    return dot(high, high, turned) + (mixed.astype(jnp.float32) + mixed.T.astype(jnp.float32))


def polynomial_step(current, norm=None):
    dot = functools.partial(lax.dot_general, preferred_element_type=jnp.float32)
    plain = (((1,), (0,)), ((), ()))
    high, low = parts_of(current)
    gram = gram_of(high, low)
    if norm is not None:
        inverse = 1.0 / norm
        gram = gram * (inverse * inverse)
    gram_high, gram_low = parts_of(gram)
    rows = current.shape[0] // 2
    blocks = []
    for k in (0, 1):
        block = slice(k * rows, (k + 1) * rows)
        square = dot(gram_high[block], gram_high, plain) + (
            dot(gram_high[block], gram_low, plain) + dot(gram_low[block], gram_high, plain)
        )
        poly_high, poly_low = parts_of(COEF_B * gram[block] + COEF_C * square)
        change = dot(poly_high, high, plain) + (
            dot(poly_high, low, plain) + dot(poly_low, high, plain)
        )
        result = COEF_A * current[block] + change
        blocks.append(result if norm is None else result * inverse)
    return jnp.concatenate(blocks, axis=0)


def ready_kernel(plan, mom_other, mom_x, mom_y, other, own, mom, base, held):
    _, c, y = here()
    half = own.shape[1]

    @pl.when(c == 0)
    def _():
        m = plan[0, 0]
        source = plan[SOURCE, 0]
        base[...] = own[m] + other[0, m]
        for part, start in enumerate((y * half, (1 - y) * half)):
            rows = pl.ds(pl.multiple_of(start, half), half)
            held[part * half : (part + 1) * half] = pick(
                [mom[rows], mom_other[0, rows], mom_x[rows], mom_y[rows]], source
            )


def nesterov_kernel(base, held, in_d, in_x, in_y, new, nesterov):
    _, c, y = here()
    half = base.shape[0]

    @pl.when(c == 0)
    def _():
        for part, start in enumerate((y * half, (1 - y) * half)):
            rows = pl.ds(pl.multiple_of(start, half), half)
            local = slice(part * half, (part + 1) * half)
            total = base[...] + in_x[...] if part == 0 else in_y[...] + in_d[...]
            buffer = MOMENT * held[local].astype(jnp.float32) + total
            new[rows] = buffer.astype(jnp.bfloat16)
            nesterov[local] = total + MOMENT * buffer


def first_kernel(steps, nesterov, after):
    _, c, _ = here()

    @pl.when(c == 0)
    def _():
        value = nesterov[...]
        squares = jnp.sum(value * value, axis=0, keepdims=True)
        norm = jnp.sqrt(jnp.sum(squares, axis=1, keepdims=True)) + 1e-07
        value = polynomial_step(value, norm)
        for _ in range(steps - 1):
            value = polynomial_step(value)
        after[...] = value


def last_kernel(steps, start, others, mine):
    _, c, _ = here()
    half = mine.shape[0]

    @pl.when(c == 0)
    def _():
        value = start[...]
        for _ in range(steps):
            value = polynomial_step(value)
        value = (FACTOR * value).astype(jnp.bfloat16)
        mine[...] = value[:half]
        others[...] = value[half:]


def place(plan, core, pieces, updates, sems):
    _, c, _ = here()

    @pl.when(c == core)
    def _():
        for k, (flip, source) in enumerate(pieces):
            pltpu.make_async_copy(source, updates.at[plan[flip, 0]], sems.at[k]).start()


def early_kernel(plan, up_d, up_l, in_d, mine, updates, sems):
    place(plan, 0, ((0, mine), (3, in_d)), updates, sems)
    place(plan, 1, ((0, up_l), (3, up_d)), updates, sems)
    for k in (0, 1):
        pltpu.make_async_copy(mine, updates.at[k], sems.at[k]).wait()


def finish_kernel(
    plan, faded, new, back, back_in, up_x, up_y, in_x, in_y, _, updates, moment, sems
):
    _, c, _ = here()
    place(plan, 0, ((2, in_x), (1, in_y)), updates, sems)
    place(plan, 1, ((2, up_x), (1, up_y)), updates, sems)
    slot = plan[SLOT, 0]
    handed = (slot == 3) & (c == 1)
    for chosen, source in (
        (slot == 0, faded),
        (slot == 1, new),
        ((slot > 1) & jnp.logical_not(handed), back),
        (handed, back_in),
    ):

        @pl.when(chosen)
        def _():
            pltpu.make_async_copy(source, moment.at[0], sems.at[2]).start()

    for k in (0, 1):
        pltpu.make_async_copy(up_x, updates.at[k], sems.at[k]).wait()
    pltpu.make_async_copy(faded, moment.at[0], sems.at[2]).wait()


def chip_device(x, c, y):
    return (2 * x + c) * 2 + y


CHIPS = [(x, y) for x in (0, 1) for y in (0, 1)]


def swap_cores(value):
    pairs = [
        (chip_device(x, c, y), chip_device(x, 1 - c, y)) for x, y in CHIPS for c in (0, 1)
    ]
    return lax.ppermute(value, AXES, pairs)


def across(value, sender, flip_x, flip_y):
    pairs = [
        (chip_device(x, sender, y), chip_device(x ^ flip_x, 1 - sender, y ^ flip_y))
        for x, y in CHIPS
    ]
    pairs += [(chip_device(x, 1 - sender, y), chip_device(x, sender, y)) for x, y in CHIPS]
    return lax.ppermute(value, AXES, pairs)


def both_ways(value):
    pairs = [(chip_device(x, 0, y), chip_device(1 - x, 1, y)) for x, y in CHIPS]
    pairs += [(chip_device(x, 1, y), chip_device(x, 0, 1 - y)) for x, y in CHIPS]
    return lax.ppermute(value, AXES, pairs)


def run(kernel, in_specs, out_shapes, out_specs=None, scratch=(), moved=0, aliases={}):
    return pl.pallas_call(
        kernel,
        in_specs=in_specs,
        out_shape=out_shapes,
        out_specs=out_specs if out_specs is not None else [VMEM] * len(out_shapes),
        scratch_shapes=list(scratch),
        input_output_aliases=aliases,
        compiler_params=pltpu.CompilerParams(vmem_limit_bytes=24 * 2**20),
        cost_estimate=pl.CostEstimate(flops=0, bytes_accessed=moved, transcendentals=0),
    )


def per_device_chips(grads, owner_slot, momentum):
    _, mats, half, width = grads.shape
    rows = momentum.shape[1]
    f32, bf16 = jnp.float32, jnp.bfloat16
    piece = jax.ShapeDtypeStruct((half, width), f32)
    whole = jax.ShapeDtypeStruct((rows, width), f32)
    moment = jax.ShapeDtypeStruct((rows, width), bf16)
    update = jax.ShapeDtypeStruct((half, width), bf16)

    near = jax.ShapeDtypeStruct((mats, half, width), f32)
    table = jax.ShapeDtypeStruct((8, 128), jnp.int32)

    mom_other = swap_cores(momentum)
    far = functools.partial(pltpu.with_memory_space_constraint, memory_space=pltpu.HBM)
    own, mom, faded, plan = run(
        load_kernel,
        [ANY] * 3,
        [near, moment, moment, table],
        scratch=[pltpu.SMEM((mats,), jnp.int32), pltpu.SemaphoreType.DMA((3,))],
        moved=2**21,
    )(far(grads), far(momentum), far(owner_slot))
    mom_other, plan, grads = lax.optimization_barrier((mom_other, plan, grads))
    grads_other = swap_cores(grads)
    (mom_out,) = run(give_kernel, [VMEM] * 3, [moment], moved=2**18)(plan, mom, mom_other)
    mom_x = across(mom_out, 1, 1, 0)
    mom_y = across(mom_out, 1, 0, 1)
    to_d, to_x, to_y = run(sum_kernel, [VMEM] * 3, [piece, piece, piece], moved=2**20)(
        plan, own, grads_other
    )
    in_d = across(to_d, 1, 1, 1)
    in_x = across(to_x, 1, 1, 0)
    in_y = across(to_y, 1, 0, 1)
    base, held = run(ready_kernel, [VMEM] * 7, [piece, moment], moved=2**20)(
        plan, mom_other, mom_x, mom_y, grads_other, own, mom
    )
    new, current = run(nesterov_kernel, [VMEM] * 5, [moment, whole], moved=2**20)(
        base, held, in_d, in_x, in_y
    )
    new_l = swap_cores(new)
    (current,) = run(functools.partial(first_kernel, 2), [VMEM], [whole], moved=2**20)(current)
    new_l, current = lax.optimization_barrier((new_l, current))
    new = jnp.where(lax.axis_index("dp") % 2 == 0, new, new_l)
    back = both_ways(new)
    others, mine = run(
        functools.partial(last_kernel, ITERS - 2), [VMEM], [update, update], moved=2**20
    )(current)
    up_d = across(others, 0, 1, 1)
    up_x = across(mine, 0, 1, 0)
    up_y = across(others, 0, 0, 1)
    up_l = swap_cores(mine)
    back_in = swap_cores(back)
    over_d, over_x, over_y = swap_cores(up_d), swap_cores(up_x), swap_cores(up_y)
    whole_updates = jax.ShapeDtypeStruct((mats, half, width), bf16)
    (updates,) = run(
        early_kernel,
        [VMEM] * 5,
        [whole_updates],
        out_specs=[ANY],
        scratch=[pltpu.SemaphoreType.DMA((2,))],
        moved=2**19,
    )(plan, up_d, up_l, over_d, mine)
    updates, new_momentum = run(
        finish_kernel,
        [VMEM] * 9 + [ANY],
        [whole_updates, jax.ShapeDtypeStruct(momentum.shape, bf16)],
        out_specs=[ANY, ANY],
        scratch=[pltpu.SemaphoreType.DMA((3,))],
        moved=2**20,
        aliases={9: 0},
    )(plan, faded, new, back, back_in, up_x, up_y, over_x, over_y, updates)
    return (updates, new_momentum)


def solution(mesh):
    placed = (P("dp", "expert", "fsdp", None), P("expert"), P(("dp", "expert", "fsdp"), None, None))
    n_replica, n_shard = mesh.shape["dp"], mesh.shape["fsdp"]

    def per_device(grads, owner_slot, momentum):
        mats, cap = grads.shape[1], momentum.shape[0]
        if (n_replica, n_shard, mats, cap) == (4, 2, 4, 1):
            return per_device_chips(grads, owner_slot, momentum)
        return per_device_general(grads, owner_slot, momentum)

    return jax.shard_map(
        per_device,
        mesh=mesh,
        in_specs=placed,
        out_specs=(P("expert", "fsdp", None), P(("dp", "expert", "fsdp"), None, None)),
        check_vma=False,
    )
```

```python
import functools
import math

import jax
import jax.numpy as jnp
from jax import lax
from jax.experimental import pallas as pl
from jax.experimental.pallas import tpu as pltpu
from jax.sharding import PartitionSpec as P

R = 256
C = 512
ITERS = 5


COEF_A = 3.4445
COEF_B = -4.775
COEF_C = 2.0315
MOMENT = 0.95
FACTOR = 0.2 * math.sqrt(max(R, C))

AXES = ("dp", "fsdp")
SMEM = pl.BlockSpec(memory_space=pltpu.SMEM)
VMEM = pl.BlockSpec(memory_space=pltpu.VMEM)
ANY = pl.BlockSpec(memory_space=pl.ANY)


def orthogonalize(stack):
    norms = jnp.sqrt(jnp.sum(stack * stack, axis=(1, 2), keepdims=True))
    current = stack / (norms + 1e-07)
    for step in range(ITERS):
        gram = jnp.einsum("krc,ksc->krs", current, current, precision=lax.Precision.HIGHEST)
        square = jnp.einsum("krs,kst->krt", gram, gram, precision=lax.Precision.HIGHEST)
        poly = COEF_B * gram + COEF_C * square
        current = COEF_A * current + jnp.einsum(
            "krs,ksc->krc", poly, current, precision=lax.Precision.HIGHEST
        )
    return current


def per_device_general(grads, owner_slot, momentum):
    partial_rows = grads[0]
    mats, rows_shard, width = partial_rows.shape
    n_replica = lax.axis_size("dp")
    n_shard = lax.axis_size("fsdp")
    owners = n_replica * n_shard
    cap = momentum.shape[0]
    rows_owner = rows_shard // n_replica
    reduced = lax.psum_scatter(partial_rows, "dp", scatter_dimension=1, tiled=True)
    slot_ids = jnp.arange(owners * cap, dtype=jnp.int32)
    matched = owner_slot[None, :] == slot_ids[:, None]
    holder = jnp.sum(jnp.where(matched, jnp.arange(mats, dtype=jnp.int32)[None, :], 0), axis=1)
    filled = jnp.any(matched, axis=1)
    outgoing = jnp.where(filled[:, None, None], jnp.take(reduced, holder, axis=0), 0.0)
    arrived = lax.all_to_all(
        outgoing.reshape(owners, cap, rows_owner, width),
        ("dp", "fsdp"),
        split_axis=0,
        concat_axis=0,
        tiled=True,
    )
    arrived = arrived.reshape(n_replica, n_shard, cap, rows_owner, width)
    whole = jnp.transpose(arrived, (2, 1, 0, 3, 4)).reshape(
        cap, n_shard * n_replica * rows_owner, width
    )
    buffer = MOMENT * momentum.astype(jnp.float32) + whole
    new_momentum = buffer.astype(jnp.bfloat16)
    nesterov = whole + MOMENT * buffer
    ortho = (FACTOR * orthogonalize(nesterov)).astype(jnp.bfloat16)
    leaving = jnp.transpose(
        ortho.reshape(cap, n_shard, n_replica, rows_owner, width), (2, 1, 0, 3, 4)
    )
    returned = lax.all_to_all(
        leaving.reshape(owners, cap, rows_owner, width),
        ("dp", "fsdp"),
        split_axis=0,
        concat_axis=0,
        tiled=True,
    )
    returned = returned.reshape(owners * cap, rows_owner, width)
    mine = jnp.take(returned, owner_slot, axis=0)
    updates = lax.all_gather(mine, "dp", axis=1, tiled=True)
    return (updates, new_momentum)


def here():
    d = lax.axis_index("dp")
    return d // 2, d % 2, lax.axis_index("fsdp")


def matrix_at(slots, chip, core):
    slot = (chip // 2) * 4 + core * 2 + chip % 2
    found = jnp.int32(-1)
    for j in range(4):
        found = jnp.where(slots[j] == slot, jnp.int32(j), found)
    return found


def deal(slots):
    at = [[matrix_at(slots, chip, core) for core in (0, 1)] for chip in range(4)]
    one, zero = jnp.int32(1), jnp.int32(0)
    extra = [
        jnp.where(at[q][0] >= 0, one, zero) + jnp.where(at[q][1] >= 0, one, zero) - 1
        for q in range(4)
    ]
    row = [extra[y] + extra[2 + y] for y in (0, 1)]
    out_y = [
        jnp.where((row[q % 2] > 0) & (extra[q ^ 1] < 0), one, zero) for q in range(4)
    ]
    out_x = [
        jnp.where(extra[q] - out_y[q] + out_y[q ^ 1] > 0, one, zero) for q in range(4)
    ]
    keep = [jnp.where(at[q][0] >= 0, at[q][0], at[q][1]) for q in range(4)]
    give = [jnp.where(at[q][1] >= 0, at[q][1], at[q][0]) for q in range(4)]
    matrix = [
        jnp.clip(
            jnp.where(
                out_y[q ^ 1] > 0, give[q ^ 1], jnp.where(out_x[q ^ 2] > 0, give[q ^ 2], keep[q])
            ),
            0,
            3,
        )
        for q in range(4)
    ]
    return at, out_x, out_y, matrix


def pick(values, index):
    result = values[0]
    for k in range(1, len(values)):
        result = jnp.where(index == k, values[k], result)
    return result


def load_kernel(
    grads, momentum, slots, grads_near, momentum_near, faded, plan, slots_near, sems
):
    copies = [
        pltpu.make_async_copy(source, target, sems.at[k])
        for k, (source, target) in enumerate(
            ((slots, slots_near), (momentum.at[0], momentum_near), (grads.at[0], grads_near))
        )
    ]
    for copy in copies:
        copy.start()
    copies[0].wait()
    x, c, y = here()
    at, out_x, out_y, matrix = deal([slots_near[j] for j in range(4)])
    q = 2 * x + y
    one, zero = jnp.int32(1), jnp.int32(0)
    at_0 = pick([at[k][0] for k in range(4)], q) >= 0
    at_1 = pick([at[k][1] for k in range(4)], q) >= 0
    leaves_x = pick(out_x, q)
    leaves_y = pick(out_y, q)
    comes_x = pick([out_x[k ^ 2] for k in range(4)], q) > 0
    comes_y = pick([out_y[k ^ 1] for k in range(4)], q) > 0
    mine = jnp.where(c == 0, at_0, at_1)
    away = jnp.where((c == 1) | jnp.logical_not(at_1), leaves_x + 2 * leaves_y, zero)
    entries = [pick([matrix[k ^ flip] for k in range(4)], q) for flip in range(4)]
    entries.append(jnp.where(comes_y, 3, jnp.where(comes_x, 2, jnp.where(at_0, zero, one))))
    entries.append(jnp.where(at_1, one, zero))
    entries.append(jnp.where(mine, one + away, zero))
    for k, entry in enumerate(entries):
        plan[k] = entry
    copies[1].wait()
    faded[...] = (MOMENT * momentum_near[...].astype(jnp.float32)).astype(jnp.bfloat16)
    copies[2].wait()


SOURCE, GIVER, SLOT = 4, 5, 6


def give_kernel(plan, mom, mom_other, mom_out):
    _, c, _ = here()

    @pl.when(c == 1)
    def _():
        mine = plan[GIVER] == 1
        mom_out[...] = jnp.where(mine, mom[...], mom_other[0])


def sum_kernel(plan, own, other, to_d, to_x, to_y):
    _, c, _ = here()

    @pl.when(c == 1)
    def _():
        for out, flip in ((to_d, 3), (to_x, 2), (to_y, 1)):
            m = plan[flip]
            out[...] = own[m] + other[0, m]


def parts_of(value):
    high = value.astype(jnp.bfloat16)
    return high, (value - high.astype(jnp.float32)).astype(jnp.bfloat16)


def gram_of(high, low):
    dot = functools.partial(lax.dot_general, preferred_element_type=jnp.float32)
    turned = (((1,), (1,)), ((), ()))
    mixed = dot(high, low, turned).astype(jnp.bfloat16)
    return dot(high, high, turned) + (mixed.astype(jnp.float32) + mixed.T.astype(jnp.float32))


def polynomial_step(current, norm=None):
    dot = functools.partial(lax.dot_general, preferred_element_type=jnp.float32)
    plain = (((1,), (0,)), ((), ()))
    high, low = parts_of(current)
    gram = gram_of(high, low)
    if norm is not None:
        inverse = 1.0 / norm
        gram = gram * (inverse * inverse)
    gram_high, gram_low = parts_of(gram)
    rows = current.shape[0] // 2
    blocks = []
    for k in (0, 1):
        block = slice(k * rows, (k + 1) * rows)
        square = dot(gram_high[block], gram_high, plain) + (
            dot(gram_high[block], gram_low, plain) + dot(gram_low[block], gram_high, plain)
        )
        poly_high, poly_low = parts_of(COEF_B * gram[block] + COEF_C * square)
        change = dot(poly_high, high, plain) + (
            dot(poly_high, low, plain) + dot(poly_low, high, plain)
        )
        result = COEF_A * current[block] + change
        blocks.append(result if norm is None else result * inverse)
    return jnp.concatenate(blocks, axis=0)


def ready_kernel(plan, mom_other, mom_x, mom_y, other, own, mom, base, held):
    _, c, y = here()
    half = own.shape[1]

    @pl.when(c == 0)
    def _():
        m = plan[0]
        source = plan[SOURCE]
        base[...] = own[m] + other[0, m]
        for part, start in enumerate((y * half, (1 - y) * half)):
            rows = pl.ds(pl.multiple_of(start, half), half)
            held[part * half : (part + 1) * half] = pick(
                [mom[rows], mom_other[0, rows], mom_x[rows], mom_y[rows]], source
            )


def nesterov_kernel(base, held, in_d, in_x, in_y, new, nesterov):
    _, c, y = here()
    half = base.shape[0]

    @pl.when(c == 0)
    def _():
        for part, start in enumerate((y * half, (1 - y) * half)):
            rows = pl.ds(pl.multiple_of(start, half), half)
            local = slice(part * half, (part + 1) * half)
            total = base[...] + in_x[...] if part == 0 else in_y[...] + in_d[...]
            buffer = MOMENT * held[local].astype(jnp.float32) + total
            new[rows] = buffer.astype(jnp.bfloat16)
            nesterov[local] = total + MOMENT * buffer


def first_kernel(steps, nesterov, after):
    _, c, _ = here()

    @pl.when(c == 0)
    def _():
        value = nesterov[...]
        squares = jnp.sum(value * value, axis=0, keepdims=True)
        norm = jnp.sqrt(jnp.sum(squares, axis=1, keepdims=True)) + 1e-07
        value = polynomial_step(value, norm)
        for _ in range(steps - 1):
            value = polynomial_step(value)
        after[...] = value


def last_kernel(steps, start, others, mine):
    _, c, _ = here()
    half = mine.shape[0]

    @pl.when(c == 0)
    def _():
        value = start[...]
        for _ in range(steps):
            value = polynomial_step(value)
        value = (FACTOR * value).astype(jnp.bfloat16)
        mine[...] = value[:half]
        others[...] = value[half:]


def place(plan, core, pieces, updates, sems):
    _, c, _ = here()

    @pl.when(c == core)
    def _():
        for k, (flip, source) in enumerate(pieces):
            pltpu.make_async_copy(source, updates.at[plan[flip]], sems.at[k]).start()


def early_kernel(plan, up_d, up_l, in_d, mine, updates, sems):
    place(plan, 0, ((0, mine), (3, in_d)), updates, sems)
    place(plan, 1, ((0, up_l), (3, up_d)), updates, sems)
    for k in (0, 1):
        pltpu.make_async_copy(mine, updates.at[k], sems.at[k]).wait()


def finish_kernel(
    plan, faded, new, back, back_in, up_x, up_y, in_x, in_y, _, updates, moment, sems
):
    _, c, _ = here()
    place(plan, 0, ((2, in_x), (1, in_y)), updates, sems)
    place(plan, 1, ((2, up_x), (1, up_y)), updates, sems)
    slot = plan[SLOT]
    handed = (slot == 3) & (c == 1)
    for chosen, source in (
        (slot == 0, faded),
        (slot == 1, new),
        ((slot > 1) & jnp.logical_not(handed), back),
        (handed, back_in),
    ):

        @pl.when(chosen)
        def _():
            pltpu.make_async_copy(source, moment.at[0], sems.at[2]).start()

    for k in (0, 1):
        pltpu.make_async_copy(up_x, updates.at[k], sems.at[k]).wait()
    pltpu.make_async_copy(faded, moment.at[0], sems.at[2]).wait()


def chip_device(x, c, y):
    return (2 * x + c) * 2 + y


CHIPS = [(x, y) for x in (0, 1) for y in (0, 1)]


def swap_cores(value):
    pairs = [
        (chip_device(x, c, y), chip_device(x, 1 - c, y)) for x, y in CHIPS for c in (0, 1)
    ]
    return lax.ppermute(value, AXES, pairs)


def across(value, sender, flip_x, flip_y):
    pairs = [
        (chip_device(x, sender, y), chip_device(x ^ flip_x, 1 - sender, y ^ flip_y))
        for x, y in CHIPS
    ]
    pairs += [(chip_device(x, 1 - sender, y), chip_device(x, sender, y)) for x, y in CHIPS]
    return lax.ppermute(value, AXES, pairs)


def both_ways(value):
    pairs = [(chip_device(x, 0, y), chip_device(1 - x, 1, y)) for x, y in CHIPS]
    pairs += [(chip_device(x, 1, y), chip_device(x, 0, 1 - y)) for x, y in CHIPS]
    return lax.ppermute(value, AXES, pairs)


def run(kernel, in_specs, out_shapes, out_specs=None, scratch=(), moved=0, aliases={}):
    return pl.pallas_call(
        kernel,
        in_specs=in_specs,
        out_shape=out_shapes,
        out_specs=out_specs if out_specs is not None else [VMEM] * len(out_shapes),
        scratch_shapes=list(scratch),
        input_output_aliases=aliases,
        compiler_params=pltpu.CompilerParams(vmem_limit_bytes=24 * 2**20),
        cost_estimate=pl.CostEstimate(flops=0, bytes_accessed=moved, transcendentals=0),
    )


def per_device_chips(grads, owner_slot, momentum):
    _, mats, half, width = grads.shape
    rows = momentum.shape[1]
    f32, bf16 = jnp.float32, jnp.bfloat16
    piece = jax.ShapeDtypeStruct((half, width), f32)
    whole = jax.ShapeDtypeStruct((rows, width), f32)
    moment = jax.ShapeDtypeStruct((rows, width), bf16)
    update = jax.ShapeDtypeStruct((half, width), bf16)

    near = jax.ShapeDtypeStruct((mats, half, width), f32)
    table = pltpu.SMEM((8,), jnp.int32)

    mom_other = swap_cores(momentum)
    far = functools.partial(pltpu.with_memory_space_constraint, memory_space=pltpu.HBM)
    own, mom, faded, plan = run(
        load_kernel,
        [ANY] * 3,
        [near, moment, moment, table],
        out_specs=[VMEM, VMEM, VMEM, SMEM],
        scratch=[pltpu.SMEM((mats,), jnp.int32), pltpu.SemaphoreType.DMA((3,))],
        moved=2**21,
    )(far(grads), far(momentum), far(owner_slot))
    plan_s = functools.partial(pltpu.with_memory_space_constraint, memory_space=pltpu.SMEM)
    mom_other, plan, grads = lax.optimization_barrier((mom_other, plan, grads))
    grads_other = swap_cores(grads)
    (mom_out,) = run(give_kernel, [SMEM] + [VMEM] * 2, [moment], moved=2**18)(plan_s(plan), mom, mom_other)
    mom_x = across(mom_out, 1, 1, 0)
    mom_y = across(mom_out, 1, 0, 1)
    to_d, to_x, to_y = run(sum_kernel, [SMEM] + [VMEM] * 2, [piece, piece, piece], moved=2**20)(
        plan_s(plan), own, grads_other
    )
    in_d = across(to_d, 1, 1, 1)
    in_x = across(to_x, 1, 1, 0)
    in_y = across(to_y, 1, 0, 1)
    base, held = run(ready_kernel, [SMEM] + [VMEM] * 6, [piece, moment], moved=2**20)(
        plan_s(plan), mom_other, mom_x, mom_y, grads_other, own, mom
    )
    new, current = run(nesterov_kernel, [VMEM] * 5, [moment, whole], moved=2**20)(
        base, held, in_d, in_x, in_y
    )
    new_l = swap_cores(new)
    (current,) = run(functools.partial(first_kernel, 2), [VMEM], [whole], moved=2**20)(current)
    new_l, current = lax.optimization_barrier((new_l, current))
    new = jnp.where(lax.axis_index("dp") % 2 == 0, new, new_l)
    back = both_ways(new)
    others, mine = run(
        functools.partial(last_kernel, ITERS - 2), [VMEM], [update, update], moved=2**20
    )(current)
    up_d = across(others, 0, 1, 1)
    up_x = across(mine, 0, 1, 0)
    up_y = across(others, 0, 0, 1)
    up_l = swap_cores(mine)
    back_in = swap_cores(back)
    over_d, over_x, over_y = swap_cores(up_d), swap_cores(up_x), swap_cores(up_y)
    whole_updates = jax.ShapeDtypeStruct((mats, half, width), bf16)
    (updates,) = run(
        early_kernel,
        [SMEM] + [VMEM] * 4,
        [whole_updates],
        out_specs=[ANY],
        scratch=[pltpu.SemaphoreType.DMA((2,))],
        moved=2**19,
    )(plan_s(plan), up_d, up_l, over_d, mine)
    updates, new_momentum = run(
        finish_kernel,
        [SMEM] + [VMEM] * 8 + [ANY],
        [whole_updates, jax.ShapeDtypeStruct(momentum.shape, bf16)],
        out_specs=[ANY, ANY],
        scratch=[pltpu.SemaphoreType.DMA((3,))],
        moved=2**20,
        aliases={9: 0},
    )(plan_s(plan), faded, new, back, back_in, up_x, up_y, over_x, over_y, updates)
    return (updates, new_momentum)


def solution(mesh):
    placed = (P("dp", "expert", "fsdp", None), P("expert"), P(("dp", "expert", "fsdp"), None, None))
    n_replica, n_shard = mesh.shape["dp"], mesh.shape["fsdp"]

    def per_device(grads, owner_slot, momentum):
        mats, cap = grads.shape[1], momentum.shape[0]
        if (n_replica, n_shard, mats, cap) == (4, 2, 4, 1):
            return per_device_chips(grads, owner_slot, momentum)
        return per_device_general(grads, owner_slot, momentum)

    return jax.shard_map(
        per_device,
        mesh=mesh,
        in_specs=placed,
        out_specs=(P("expert", "fsdp", None), P(("dp", "expert", "fsdp"), None, None)),
        check_vma=False,
    )
```

```python
import functools
import math

import jax
import jax.numpy as jnp
from jax import lax
from jax.experimental import pallas as pl
from jax.experimental.pallas import tpu as pltpu
from jax.sharding import PartitionSpec as P

R = 256
C = 512
ITERS = 5


COEF_A = 3.4445
COEF_B = -4.775
COEF_C = 2.0315
MOMENT = 0.95
FACTOR = 0.2 * math.sqrt(max(R, C))

AXES = ("dp", "fsdp")
SMEM = pl.BlockSpec(memory_space=pltpu.SMEM)
VMEM = pl.BlockSpec(memory_space=pltpu.VMEM)
ANY = pl.BlockSpec(memory_space=pl.ANY)


def orthogonalize(stack):
    norms = jnp.sqrt(jnp.sum(stack * stack, axis=(1, 2), keepdims=True))
    current = stack / (norms + 1e-07)
    for step in range(ITERS):
        gram = jnp.einsum("krc,ksc->krs", current, current, precision=lax.Precision.HIGHEST)
        square = jnp.einsum("krs,kst->krt", gram, gram, precision=lax.Precision.HIGHEST)
        poly = COEF_B * gram + COEF_C * square
        current = COEF_A * current + jnp.einsum(
            "krs,ksc->krc", poly, current, precision=lax.Precision.HIGHEST
        )
    return current


def per_device_general(grads, owner_slot, momentum):
    partial_rows = grads[0]
    mats, rows_shard, width = partial_rows.shape
    n_replica = lax.axis_size("dp")
    n_shard = lax.axis_size("fsdp")
    owners = n_replica * n_shard
    cap = momentum.shape[0]
    rows_owner = rows_shard // n_replica
    reduced = lax.psum_scatter(partial_rows, "dp", scatter_dimension=1, tiled=True)
    slot_ids = jnp.arange(owners * cap, dtype=jnp.int32)
    matched = owner_slot[None, :] == slot_ids[:, None]
    holder = jnp.sum(jnp.where(matched, jnp.arange(mats, dtype=jnp.int32)[None, :], 0), axis=1)
    filled = jnp.any(matched, axis=1)
    outgoing = jnp.where(filled[:, None, None], jnp.take(reduced, holder, axis=0), 0.0)
    arrived = lax.all_to_all(
        outgoing.reshape(owners, cap, rows_owner, width),
        ("dp", "fsdp"),
        split_axis=0,
        concat_axis=0,
        tiled=True,
    )
    arrived = arrived.reshape(n_replica, n_shard, cap, rows_owner, width)
    whole = jnp.transpose(arrived, (2, 1, 0, 3, 4)).reshape(
        cap, n_shard * n_replica * rows_owner, width
    )
    buffer = MOMENT * momentum.astype(jnp.float32) + whole
    new_momentum = buffer.astype(jnp.bfloat16)
    nesterov = whole + MOMENT * buffer
    ortho = (FACTOR * orthogonalize(nesterov)).astype(jnp.bfloat16)
    leaving = jnp.transpose(
        ortho.reshape(cap, n_shard, n_replica, rows_owner, width), (2, 1, 0, 3, 4)
    )
    returned = lax.all_to_all(
        leaving.reshape(owners, cap, rows_owner, width),
        ("dp", "fsdp"),
        split_axis=0,
        concat_axis=0,
        tiled=True,
    )
    returned = returned.reshape(owners * cap, rows_owner, width)
    mine = jnp.take(returned, owner_slot, axis=0)
    updates = lax.all_gather(mine, "dp", axis=1, tiled=True)
    return (updates, new_momentum)


def here():
    d = lax.axis_index("dp")
    return d // 2, d % 2, lax.axis_index("fsdp")


def matrix_at(slots, chip, core):
    slot = (chip // 2) * 4 + core * 2 + chip % 2
    found = jnp.int32(-1)
    for j in range(4):
        found = jnp.where(slots[j] == slot, jnp.int32(j), found)
    return found


def deal(slots):
    at = [[matrix_at(slots, chip, core) for core in (0, 1)] for chip in range(4)]
    one, zero = jnp.int32(1), jnp.int32(0)
    extra = [
        jnp.where(at[q][0] >= 0, one, zero) + jnp.where(at[q][1] >= 0, one, zero) - 1
        for q in range(4)
    ]
    row = [extra[y] + extra[2 + y] for y in (0, 1)]
    out_y = [
        jnp.where((row[q % 2] > 0) & (extra[q ^ 1] < 0), one, zero) for q in range(4)
    ]
    out_x = [
        jnp.where(extra[q] - out_y[q] + out_y[q ^ 1] > 0, one, zero) for q in range(4)
    ]
    keep = [jnp.where(at[q][0] >= 0, at[q][0], at[q][1]) for q in range(4)]
    give = [jnp.where(at[q][1] >= 0, at[q][1], at[q][0]) for q in range(4)]
    matrix = [
        jnp.clip(
            jnp.where(
                out_y[q ^ 1] > 0, give[q ^ 1], jnp.where(out_x[q ^ 2] > 0, give[q ^ 2], keep[q])
            ),
            0,
            3,
        )
        for q in range(4)
    ]
    return at, out_x, out_y, matrix


def pick(values, index):
    result = values[0]
    for k in range(1, len(values)):
        result = jnp.where(index == k, values[k], result)
    return result


def load_kernel(
    grads, momentum, slots, grads_near, momentum_near, faded, plan, slots_near, sems
):
    copies = [
        pltpu.make_async_copy(source, target, sems.at[k])
        for k, (source, target) in enumerate(
            ((slots, slots_near), (momentum.at[0], momentum_near), (grads.at[0], grads_near))
        )
    ]
    for copy in copies:
        copy.start()
    copies[0].wait()
    x, c, y = here()
    at, out_x, out_y, matrix = deal([slots_near[j] for j in range(4)])
    q = 2 * x + y
    one, zero = jnp.int32(1), jnp.int32(0)
    at_0 = pick([at[k][0] for k in range(4)], q) >= 0
    at_1 = pick([at[k][1] for k in range(4)], q) >= 0
    leaves_x = pick(out_x, q)
    leaves_y = pick(out_y, q)
    comes_x = pick([out_x[k ^ 2] for k in range(4)], q) > 0
    comes_y = pick([out_y[k ^ 1] for k in range(4)], q) > 0
    mine = jnp.where(c == 0, at_0, at_1)
    away = jnp.where((c == 1) | jnp.logical_not(at_1), leaves_x + 2 * leaves_y, zero)
    entries = [pick([matrix[k ^ flip] for k in range(4)], q) for flip in range(4)]
    entries.append(jnp.where(comes_y, 3, jnp.where(comes_x, 2, jnp.where(at_0, zero, one))))
    entries.append(jnp.where(at_1, one, zero))
    entries.append(jnp.where(mine, one + away, zero))
    for k, entry in enumerate(entries):
        plan[k] = entry
    copies[1].wait()
    faded[...] = (MOMENT * momentum_near[...].astype(jnp.float32)).astype(jnp.bfloat16)
    copies[2].wait()


SOURCE, GIVER, SLOT = 4, 5, 6


def give_kernel(plan, mom, mom_other, mom_out):
    _, c, _ = here()

    @pl.when(c == 1)
    def _():
        mine = plan[GIVER] == 1
        mom_out[...] = jnp.where(mine, mom[...], mom_other[0])


def sum_kernel(plan, own, other, to_d, to_x, to_y):
    _, c, _ = here()

    @pl.when(c == 1)
    def _():
        for out, flip in ((to_d, 3), (to_x, 2), (to_y, 1)):
            m = plan[flip]
            out[...] = own[m] + other[m]


def parts_of(value):
    high = value.astype(jnp.bfloat16)
    return high, (value - high.astype(jnp.float32)).astype(jnp.bfloat16)


def gram_of(high, low):
    dot = functools.partial(lax.dot_general, preferred_element_type=jnp.float32)
    turned = (((1,), (1,)), ((), ()))
    main = dot(high, high, turned)
    mixed = dot(high, low, turned).astype(jnp.bfloat16)
    return main + (mixed.astype(jnp.float32) + mixed.T.astype(jnp.float32))


def polynomial_step(current, norm=None):
    dot = functools.partial(lax.dot_general, preferred_element_type=jnp.float32)
    plain = (((1,), (0,)), ((), ()))
    high, low = parts_of(current)
    gram = gram_of(high, low)
    if norm is not None:
        inverse = 1.0 / norm
        gram = gram * (inverse * inverse)
    gram_high, gram_low = parts_of(gram)
    rows = current.shape[0] // 2
    blocks = []
    for k in (0, 1):
        block = slice(k * rows, (k + 1) * rows)
        square = dot(gram_high[block], gram_high, plain) + (
            dot(gram_high[block], gram_low, plain) + dot(gram_low[block], gram_high, plain)
        )
        poly_high, poly_low = parts_of(COEF_B * gram[block] + COEF_C * square)
        change = dot(poly_high, high, plain) + (
            dot(poly_high, low, plain) + dot(poly_low, high, plain)
        )
        result = COEF_A * current[block] + change
        blocks.append(result if norm is None else result * inverse)
    return jnp.concatenate(blocks, axis=0)


def ready_kernel(plan, mom_other, mom_x, mom_y, other, own, mom, base, held):
    _, c, y = here()
    half = own.shape[1]

    @pl.when(c == 0)
    def _():
        m = plan[0]
        source = plan[SOURCE]
        base[...] = own[m] + other[m]
        for part, start in enumerate((y * half, (1 - y) * half)):
            rows = pl.ds(pl.multiple_of(start, half), half)
            held[part * half : (part + 1) * half] = pick(
                [mom[rows], mom_other[0, rows], mom_x[rows], mom_y[rows]], source
            )


def nesterov_kernel(base, held, in_d, in_x, in_y, new, nesterov):
    _, c, y = here()
    half = base.shape[0]

    @pl.when(c == 0)
    def _():
        for part, start in enumerate((y * half, (1 - y) * half)):
            rows = pl.ds(pl.multiple_of(start, half), half)
            local = slice(part * half, (part + 1) * half)
            total = base[...] + in_x[...] if part == 0 else in_y[...] + in_d[...]
            buffer = MOMENT * held[local].astype(jnp.float32) + total
            new[rows] = buffer.astype(jnp.bfloat16)
            nesterov[local] = total + MOMENT * buffer


def first_kernel(steps, nesterov, after):
    _, c, _ = here()

    @pl.when(c == 0)
    def _():
        value = nesterov[...]
        squares = jnp.sum(value * value, axis=0, keepdims=True)
        norm = jnp.sqrt(jnp.sum(squares, axis=1, keepdims=True)) + 1e-07
        value = polynomial_step(value, norm)
        for _ in range(steps - 1):
            value = polynomial_step(value)
        after[...] = value


def last_kernel(steps, start, others, mine):
    _, c, _ = here()
    half = mine.shape[0]

    @pl.when(c == 0)
    def _():
        value = start[...]
        for _ in range(steps):
            value = polynomial_step(value)
        value = (FACTOR * value).astype(jnp.bfloat16)
        mine[...] = value[:half]
        others[...] = value[half:]


def place(plan, core, pieces, updates, sems):
    _, c, _ = here()

    @pl.when(c == core)
    def _():
        for k, (flip, source) in enumerate(pieces):
            pltpu.make_async_copy(source, updates.at[plan[flip]], sems.at[k]).start()


def early_kernel(plan, up_d, up_l, in_d, mine, updates, sems):
    place(plan, 0, ((0, mine), (3, in_d)), updates, sems)
    place(plan, 1, ((0, up_l), (3, up_d)), updates, sems)
    for k in (0, 1):
        pltpu.make_async_copy(mine, updates.at[k], sems.at[k]).wait()


def finish_kernel(
    plan, faded, new, back, back_in, up_x, up_y, in_x, in_y, _, updates, moment, sems
):
    _, c, _ = here()
    place(plan, 0, ((2, in_x), (1, in_y)), updates, sems)
    place(plan, 1, ((2, up_x), (1, up_y)), updates, sems)
    slot = plan[SLOT]
    handed = (slot == 3) & (c == 1)
    for chosen, source in (
        (slot == 0, faded),
        (slot == 1, new),
        ((slot > 1) & jnp.logical_not(handed), back),
        (handed, back_in),
    ):

        @pl.when(chosen)
        def _():
            pltpu.make_async_copy(source, moment.at[0], sems.at[2]).start()

    for k in (0, 1):
        pltpu.make_async_copy(up_x, updates.at[k], sems.at[k]).wait()
    pltpu.make_async_copy(faded, moment.at[0], sems.at[2]).wait()


def chip_device(x, c, y):
    return (2 * x + c) * 2 + y


CHIPS = [(x, y) for x in (0, 1) for y in (0, 1)]


def swap_cores(value):
    pairs = [
        (chip_device(x, c, y), chip_device(x, 1 - c, y)) for x, y in CHIPS for c in (0, 1)
    ]
    return lax.ppermute(value, AXES, pairs)


def across(value, sender, flip_x, flip_y):
    pairs = [
        (chip_device(x, sender, y), chip_device(x ^ flip_x, 1 - sender, y ^ flip_y))
        for x, y in CHIPS
    ]
    pairs += [(chip_device(x, 1 - sender, y), chip_device(x, sender, y)) for x, y in CHIPS]
    return lax.ppermute(value, AXES, pairs)


def both_ways(value):
    pairs = [(chip_device(x, 0, y), chip_device(1 - x, 1, y)) for x, y in CHIPS]
    pairs += [(chip_device(x, 1, y), chip_device(x, 0, 1 - y)) for x, y in CHIPS]
    return lax.ppermute(value, AXES, pairs)


def run(kernel, in_specs, out_shapes, out_specs=None, scratch=(), moved=0, aliases={}):
    return pl.pallas_call(
        kernel,
        in_specs=in_specs,
        out_shape=out_shapes,
        out_specs=out_specs if out_specs is not None else [VMEM] * len(out_shapes),
        scratch_shapes=list(scratch),
        input_output_aliases=aliases,
        compiler_params=pltpu.CompilerParams(vmem_limit_bytes=24 * 2**20),
        cost_estimate=pl.CostEstimate(flops=0, bytes_accessed=moved, transcendentals=0),
    )


def per_device_chips(grads, owner_slot, momentum):
    _, mats, half, width = grads.shape
    rows = momentum.shape[1]
    f32, bf16 = jnp.float32, jnp.bfloat16
    piece = jax.ShapeDtypeStruct((half, width), f32)
    whole = jax.ShapeDtypeStruct((rows, width), f32)
    moment = jax.ShapeDtypeStruct((rows, width), bf16)
    update = jax.ShapeDtypeStruct((half, width), bf16)

    near = jax.ShapeDtypeStruct((mats, half, width), f32)
    table = pltpu.SMEM((8,), jnp.int32)

    mom_other = swap_cores(momentum)
    far = functools.partial(pltpu.with_memory_space_constraint, memory_space=pltpu.HBM)
    own, mom, faded, plan = run(
        load_kernel,
        [ANY] * 3,
        [near, moment, moment, table],
        out_specs=[VMEM, VMEM, VMEM, SMEM],
        scratch=[pltpu.SMEM((mats,), jnp.int32), pltpu.SemaphoreType.DMA((3,))],
        moved=2**21,
    )(far(grads), far(momentum), far(owner_slot))
    plan_s = functools.partial(pltpu.with_memory_space_constraint, memory_space=pltpu.SMEM)
    mom_other, plan, own = lax.optimization_barrier((mom_other, plan, own))
    grads_other = swap_cores(own)
    (mom_out,) = run(give_kernel, [SMEM] + [VMEM] * 2, [moment], moved=2**18)(plan_s(plan), mom, mom_other)
    mom_x = across(mom_out, 1, 1, 0)
    mom_y = across(mom_out, 1, 0, 1)
    to_d, to_x, to_y = run(sum_kernel, [SMEM] + [VMEM] * 2, [piece, piece, piece], moved=2**20)(
        plan_s(plan), own, grads_other
    )
    in_d = across(to_d, 1, 1, 1)
    in_x = across(to_x, 1, 1, 0)
    in_y = across(to_y, 1, 0, 1)
    base, held = run(ready_kernel, [SMEM] + [VMEM] * 6, [piece, moment], moved=2**20)(
        plan_s(plan), mom_other, mom_x, mom_y, grads_other, own, mom
    )
    new, current = run(nesterov_kernel, [VMEM] * 5, [moment, whole], moved=2**20)(
        base, held, in_d, in_x, in_y
    )
    new_l = swap_cores(new)
    (current,) = run(functools.partial(first_kernel, 2), [VMEM], [whole], moved=2**20)(current)
    new_l, current = lax.optimization_barrier((new_l, current))
    new = jnp.where(lax.axis_index("dp") % 2 == 0, new, new_l)
    back = both_ways(new)
    others, mine = run(
        functools.partial(last_kernel, ITERS - 2), [VMEM], [update, update], moved=2**20
    )(current)
    up_d = across(others, 0, 1, 1)
    up_x = across(mine, 0, 1, 0)
    up_y = across(others, 0, 0, 1)
    up_l = swap_cores(mine)
    back_in = swap_cores(back)
    over_d, over_x, over_y = swap_cores(up_d), swap_cores(up_x), swap_cores(up_y)
    whole_updates = jax.ShapeDtypeStruct((mats, half, width), bf16)
    (updates,) = run(
        early_kernel,
        [SMEM] + [VMEM] * 4,
        [whole_updates],
        out_specs=[ANY],
        scratch=[pltpu.SemaphoreType.DMA((2,))],
        moved=2**19,
    )(plan_s(plan), up_d, up_l, over_d, mine)
    updates, new_momentum = run(
        finish_kernel,
        [SMEM] + [VMEM] * 8 + [ANY],
        [whole_updates, jax.ShapeDtypeStruct(momentum.shape, bf16)],
        out_specs=[ANY, ANY],
        scratch=[pltpu.SemaphoreType.DMA((3,))],
        moved=2**20,
        aliases={9: 0},
    )(plan_s(plan), faded, new, back, back_in, up_x, up_y, over_x, over_y, updates)
    return (updates, new_momentum)


def solution(mesh):
    placed = (P("dp", "expert", "fsdp", None), P("expert"), P(("dp", "expert", "fsdp"), None, None))
    n_replica, n_shard = mesh.shape["dp"], mesh.shape["fsdp"]

    def per_device(grads, owner_slot, momentum):
        mats, cap = grads.shape[1], momentum.shape[0]
        if (n_replica, n_shard, mats, cap) == (4, 2, 4, 1):
            return per_device_chips(grads, owner_slot, momentum)
        return per_device_general(grads, owner_slot, momentum)

    return jax.shard_map(
        per_device,
        mesh=mesh,
        in_specs=placed,
        out_specs=(P("expert", "fsdp", None), P(("dp", "expert", "fsdp"), None, None)),
        check_vma=False,
    )
```

```python
import functools
import math

import jax
import jax.numpy as jnp
from jax import lax
from jax.experimental import pallas as pl
from jax.experimental.pallas import tpu as pltpu
from jax.sharding import PartitionSpec as P

R = 256
C = 512
ITERS = 5


COEF_A = 3.4445
COEF_B = -4.775
COEF_C = 2.0315
MOMENT = 0.95
FACTOR = 0.2 * math.sqrt(max(R, C))

AXES = ("dp", "fsdp")
SMEM = pl.BlockSpec(memory_space=pltpu.SMEM)
VMEM = pl.BlockSpec(memory_space=pltpu.VMEM)
ANY = pl.BlockSpec(memory_space=pl.ANY)


def orthogonalize(stack):
    norms = jnp.sqrt(jnp.sum(stack * stack, axis=(1, 2), keepdims=True))
    current = stack / (norms + 1e-07)
    for step in range(ITERS):
        gram = jnp.einsum("krc,ksc->krs", current, current, precision=lax.Precision.HIGHEST)
        square = jnp.einsum("krs,kst->krt", gram, gram, precision=lax.Precision.HIGHEST)
        poly = COEF_B * gram + COEF_C * square
        current = COEF_A * current + jnp.einsum(
            "krs,ksc->krc", poly, current, precision=lax.Precision.HIGHEST
        )
    return current


def per_device_general(grads, owner_slot, momentum):
    partial_rows = grads[0]
    mats, rows_shard, width = partial_rows.shape
    n_replica = lax.axis_size("dp")
    n_shard = lax.axis_size("fsdp")
    owners = n_replica * n_shard
    cap = momentum.shape[0]
    rows_owner = rows_shard // n_replica
    reduced = lax.psum_scatter(partial_rows, "dp", scatter_dimension=1, tiled=True)
    slot_ids = jnp.arange(owners * cap, dtype=jnp.int32)
    matched = owner_slot[None, :] == slot_ids[:, None]
    holder = jnp.sum(jnp.where(matched, jnp.arange(mats, dtype=jnp.int32)[None, :], 0), axis=1)
    filled = jnp.any(matched, axis=1)
    outgoing = jnp.where(filled[:, None, None], jnp.take(reduced, holder, axis=0), 0.0)
    arrived = lax.all_to_all(
        outgoing.reshape(owners, cap, rows_owner, width),
        ("dp", "fsdp"),
        split_axis=0,
        concat_axis=0,
        tiled=True,
    )
    arrived = arrived.reshape(n_replica, n_shard, cap, rows_owner, width)
    whole = jnp.transpose(arrived, (2, 1, 0, 3, 4)).reshape(
        cap, n_shard * n_replica * rows_owner, width
    )
    buffer = MOMENT * momentum.astype(jnp.float32) + whole
    new_momentum = buffer.astype(jnp.bfloat16)
    nesterov = whole + MOMENT * buffer
    ortho = (FACTOR * orthogonalize(nesterov)).astype(jnp.bfloat16)
    leaving = jnp.transpose(
        ortho.reshape(cap, n_shard, n_replica, rows_owner, width), (2, 1, 0, 3, 4)
    )
    returned = lax.all_to_all(
        leaving.reshape(owners, cap, rows_owner, width),
        ("dp", "fsdp"),
        split_axis=0,
        concat_axis=0,
        tiled=True,
    )
    returned = returned.reshape(owners * cap, rows_owner, width)
    mine = jnp.take(returned, owner_slot, axis=0)
    updates = lax.all_gather(mine, "dp", axis=1, tiled=True)
    return (updates, new_momentum)


def here():
    d = lax.axis_index("dp")
    return d // 2, d % 2, lax.axis_index("fsdp")


def matrix_at(slots, chip, core):
    slot = (chip // 2) * 4 + core * 2 + chip % 2
    found = jnp.int32(-1)
    for j in range(4):
        found = jnp.where(slots[j] == slot, jnp.int32(j), found)
    return found


def deal(slots):
    at = [[matrix_at(slots, chip, core) for core in (0, 1)] for chip in range(4)]
    one, zero = jnp.int32(1), jnp.int32(0)
    extra = [
        jnp.where(at[q][0] >= 0, one, zero) + jnp.where(at[q][1] >= 0, one, zero) - 1
        for q in range(4)
    ]
    row = [extra[y] + extra[2 + y] for y in (0, 1)]
    out_y = [
        jnp.where((row[q % 2] > 0) & (extra[q ^ 1] < 0), one, zero) for q in range(4)
    ]
    out_x = [
        jnp.where(extra[q] - out_y[q] + out_y[q ^ 1] > 0, one, zero) for q in range(4)
    ]
    keep = [jnp.where(at[q][0] >= 0, at[q][0], at[q][1]) for q in range(4)]
    give = [jnp.where(at[q][1] >= 0, at[q][1], at[q][0]) for q in range(4)]
    matrix = [
        jnp.clip(
            jnp.where(
                out_y[q ^ 1] > 0, give[q ^ 1], jnp.where(out_x[q ^ 2] > 0, give[q ^ 2], keep[q])
            ),
            0,
            3,
        )
        for q in range(4)
    ]
    return at, out_x, out_y, matrix


def pick(values, index):
    result = values[0]
    for k in range(1, len(values)):
        result = jnp.where(index == k, values[k], result)
    return result


def load_kernel(
    grads, momentum, slots, grads_near, momentum_near, faded, plan, slots_near, sems
):
    copies = [
        pltpu.make_async_copy(source, target, sems.at[k])
        for k, (source, target) in enumerate(
            ((slots, slots_near), (momentum.at[0], momentum_near), (grads.at[0], grads_near))
        )
    ]
    for copy in copies:
        copy.start()
    copies[0].wait()
    x, c, y = here()
    at, out_x, out_y, matrix = deal([slots_near[j] for j in range(4)])
    q = 2 * x + y
    one, zero = jnp.int32(1), jnp.int32(0)
    at_0 = pick([at[k][0] for k in range(4)], q) >= 0
    at_1 = pick([at[k][1] for k in range(4)], q) >= 0
    leaves_x = pick(out_x, q)
    leaves_y = pick(out_y, q)
    comes_x = pick([out_x[k ^ 2] for k in range(4)], q) > 0
    comes_y = pick([out_y[k ^ 1] for k in range(4)], q) > 0
    mine = jnp.where(c == 0, at_0, at_1)
    away = jnp.where((c == 1) | jnp.logical_not(at_1), leaves_x + 2 * leaves_y, zero)
    entries = [pick([matrix[k ^ flip] for k in range(4)], q) for flip in range(4)]
    entries.append(jnp.where(comes_y, 3, jnp.where(comes_x, 2, jnp.where(at_0, zero, one))))
    entries.append(jnp.where(at_1, one, zero))
    entries.append(jnp.where(mine, one + away, zero))
    for k, entry in enumerate(entries):
        plan[k] = entry
    copies[1].wait()
    faded[...] = (MOMENT * momentum_near[...].astype(jnp.float32)).astype(jnp.bfloat16)
    copies[2].wait()


SOURCE, GIVER, SLOT = 4, 5, 6


def give_kernel(plan, mom, mom_other, mom_out):
    _, c, _ = here()

    @pl.when(c == 1)
    def _():
        mine = plan[GIVER] == 1
        mom_out[...] = jnp.where(mine, mom[...], mom_other[0])


def sum_kernel(plan, own, other, to_d, to_x, to_y):
    _, c, _ = here()

    @pl.when(c == 1)
    def _():
        for out, flip in ((to_d, 3), (to_x, 2), (to_y, 1)):
            m = plan[flip]
            out[...] = own[m] + other[m]


def parts_of(value):
    high = value.astype(jnp.bfloat16)
    return high, (value - high.astype(jnp.float32)).astype(jnp.bfloat16)


def gram_of(high, low):
    dot = functools.partial(lax.dot_general, preferred_element_type=jnp.float32)
    turned = (((1,), (1,)), ((), ()))
    main = dot(high, high, turned)
    mixed = dot(high, low, turned).astype(jnp.bfloat16)
    return main + (mixed.astype(jnp.float32) + mixed.T.astype(jnp.float32))


def polynomial_step(current, norm=None):
    dot = functools.partial(lax.dot_general, preferred_element_type=jnp.float32)
    plain = (((1,), (0,)), ((), ()))
    high, low = parts_of(current)
    gram = gram_of(high, low)
    if norm is not None:
        inverse = 1.0 / norm
        gram = gram * (inverse * inverse)
    gram_high, gram_low = parts_of(gram)
    rows = current.shape[0] // 2
    blocks = []
    for k in (0, 1):
        block = slice(k * rows, (k + 1) * rows)
        square = dot(gram_high[block], gram_high, plain) + (
            dot(gram_high[block], gram_low, plain) + dot(gram_low[block], gram_high, plain)
        )
        poly_high, poly_low = parts_of(COEF_B * gram[block] + COEF_C * square)
        change = dot(poly_high, high, plain) + (
            dot(poly_high, low, plain) + dot(poly_low, high, plain)
        )
        result = COEF_A * current[block] + change
        blocks.append(result if norm is None else result * inverse)
    return jnp.concatenate(blocks, axis=0)


def ready_kernel(plan, mom_other, mom_x, mom_y, other, own, mom, base, held):
    _, c, y = here()
    half = own.shape[1]

    @pl.when(c == 0)
    def _():
        m = plan[0]
        source = plan[SOURCE]
        base[...] = own[m] + other[m]
        for part, start in enumerate((y * half, (1 - y) * half)):
            rows = pl.ds(pl.multiple_of(start, half), half)
            held[part * half : (part + 1) * half] = pick(
                [mom[rows], mom_other[0, rows], mom_x[rows], mom_y[rows]], source
            )


def nesterov_kernel(base, held, in_d, in_x, in_y, new, nesterov):
    _, c, y = here()
    half = base.shape[0]

    @pl.when(c == 0)
    def _():
        for part, start in enumerate((y * half, (1 - y) * half)):
            rows = pl.ds(pl.multiple_of(start, half), half)
            local = slice(part * half, (part + 1) * half)
            total = base[...] + in_x[...] if part == 0 else in_y[...] + in_d[...]
            buffer = MOMENT * held[local].astype(jnp.float32) + total
            new[rows] = buffer.astype(jnp.bfloat16)
            nesterov[local] = total + MOMENT * buffer


def first_kernel(steps, nesterov, after):
    _, c, _ = here()

    @pl.when(c == 0)
    def _():
        value = nesterov[...]
        squares = jnp.sum(value * value, axis=0, keepdims=True)
        norm = jnp.sqrt(jnp.sum(squares, axis=1, keepdims=True)) + 1e-07
        value = polynomial_step(value, norm)
        for _ in range(steps - 1):
            value = polynomial_step(value)
        after[...] = value


def last_kernel(steps, start, others, mine):
    _, c, _ = here()
    half = mine.shape[0]

    @pl.when(c == 0)
    def _():
        value = start[...]
        for _ in range(steps):
            value = polynomial_step(value)
        value = (FACTOR * value).astype(jnp.bfloat16)
        mine[...] = value[:half]
        others[...] = value[half:]


def place(plan, core, pieces, updates, sems):
    _, c, _ = here()

    @pl.when(c == core)
    def _():
        for k, (flip, source) in enumerate(pieces):
            pltpu.make_async_copy(source, updates.at[plan[flip]], sems.at[k]).start()


def early_kernel(plan, up_d, up_l, in_d, mine, updates, sems):
    place(plan, 0, ((0, mine), (3, in_d)), updates, sems)
    place(plan, 1, ((0, up_l), (3, up_d)), updates, sems)
    for k in (0, 1):
        pltpu.make_async_copy(mine, updates.at[k], sems.at[k]).wait()


def finish_kernel(
    plan, faded, new, back, back_in, up_x, up_y, in_x, in_y, _, updates, moment, sems
):
    _, c, _ = here()
    place(plan, 0, ((2, in_x), (1, in_y)), updates, sems)
    place(plan, 1, ((2, up_x), (1, up_y)), updates, sems)
    slot = plan[SLOT]
    handed = (slot == 3) & (c == 1)
    for chosen, source in (
        (slot == 0, faded),
        (slot == 1, new),
        ((slot > 1) & jnp.logical_not(handed), back),
        (handed, back_in),
    ):

        @pl.when(chosen)
        def _():
            pltpu.make_async_copy(source, moment.at[0], sems.at[2]).start()

    for k in (0, 1):
        pltpu.make_async_copy(up_x, updates.at[k], sems.at[k]).wait()
    pltpu.make_async_copy(faded, moment.at[0], sems.at[2]).wait()


def chip_device(x, c, y):
    return (2 * x + c) * 2 + y


CHIPS = [(x, y) for x in (0, 1) for y in (0, 1)]


def swap_cores(value):
    pairs = [
        (chip_device(x, c, y), chip_device(x, 1 - c, y)) for x, y in CHIPS for c in (0, 1)
    ]
    return lax.ppermute(value, AXES, pairs)


def across(value, sender, flip_x, flip_y):
    pairs = [
        (chip_device(x, sender, y), chip_device(x ^ flip_x, 1 - sender, y ^ flip_y))
        for x, y in CHIPS
    ]
    pairs += [(chip_device(x, 1 - sender, y), chip_device(x, sender, y)) for x, y in CHIPS]
    return lax.ppermute(value, AXES, pairs)


def both_ways(value):
    pairs = [(chip_device(x, 0, y), chip_device(1 - x, 1, y)) for x, y in CHIPS]
    pairs += [(chip_device(x, 1, y), chip_device(x, 0, 1 - y)) for x, y in CHIPS]
    return lax.ppermute(value, AXES, pairs)


def run(kernel, in_specs, out_shapes, out_specs=None, scratch=(), moved=0, aliases={}):
    return pl.pallas_call(
        kernel,
        in_specs=in_specs,
        out_shape=out_shapes,
        out_specs=out_specs if out_specs is not None else [VMEM] * len(out_shapes),
        scratch_shapes=list(scratch),
        input_output_aliases=aliases,
        compiler_params=pltpu.CompilerParams(vmem_limit_bytes=24 * 2**20),
        cost_estimate=pl.CostEstimate(flops=0, bytes_accessed=moved, transcendentals=0),
    )


def per_device_chips(grads, owner_slot, momentum):
    _, mats, half, width = grads.shape
    rows = momentum.shape[1]
    f32, bf16 = jnp.float32, jnp.bfloat16
    piece = jax.ShapeDtypeStruct((half, width), f32)
    whole = jax.ShapeDtypeStruct((rows, width), f32)
    moment = jax.ShapeDtypeStruct((rows, width), bf16)
    update = jax.ShapeDtypeStruct((half, width), bf16)

    near = jax.ShapeDtypeStruct((mats, half, width), f32)
    table = pltpu.SMEM((8,), jnp.int32)

    mom_other = swap_cores(momentum)
    far = functools.partial(pltpu.with_memory_space_constraint, memory_space=pltpu.HBM)
    own, mom, faded, plan = run(
        load_kernel,
        [ANY] * 3,
        [near, moment, moment, table],
        out_specs=[VMEM, VMEM, VMEM, SMEM],
        scratch=[pltpu.SMEM((mats,), jnp.int32), pltpu.SemaphoreType.DMA((3,))],
        moved=2**21,
    )(far(grads), far(momentum), far(owner_slot))
    plan_s = functools.partial(pltpu.with_memory_space_constraint, memory_space=pltpu.SMEM)
    mom_other, plan, own = lax.optimization_barrier((mom_other, plan, own))
    grads_other = swap_cores(own)
    (mom_out,) = run(give_kernel, [SMEM] + [VMEM] * 2, [moment], moved=2**18)(plan_s(plan), mom, mom_other)
    mom_x = across(mom, 1, 1, 0)
    mom_y = across(mom_out, 1, 0, 1)
    to_d, to_x, to_y = run(sum_kernel, [SMEM] + [VMEM] * 2, [piece, piece, piece], moved=2**20)(
        plan_s(plan), own, grads_other
    )
    in_d = across(to_d, 1, 1, 1)
    in_x = across(to_x, 1, 1, 0)
    in_y = across(to_y, 1, 0, 1)
    base, held = run(ready_kernel, [SMEM] + [VMEM] * 6, [piece, moment], moved=2**20)(
        plan_s(plan), mom_other, mom_x, mom_y, grads_other, own, mom
    )
    new, current = run(nesterov_kernel, [VMEM] * 5, [moment, whole], moved=2**20)(
        base, held, in_d, in_x, in_y
    )
    new_l = swap_cores(new)
    (current,) = run(functools.partial(first_kernel, 2), [VMEM], [whole], moved=2**20)(current)
    new_l, current = lax.optimization_barrier((new_l, current))
    new = jnp.where(lax.axis_index("dp") % 2 == 0, new, new_l)
    back = both_ways(new)
    others, mine = run(
        functools.partial(last_kernel, ITERS - 2), [VMEM], [update, update], moved=2**20
    )(current)
    up_d = across(others, 0, 1, 1)
    up_x = across(mine, 0, 1, 0)
    up_y = across(others, 0, 0, 1)
    up_l = swap_cores(mine)
    back_in = swap_cores(back)
    over_d, over_x, over_y = swap_cores(up_d), swap_cores(up_x), swap_cores(up_y)
    whole_updates = jax.ShapeDtypeStruct((mats, half, width), bf16)
    (updates,) = run(
        early_kernel,
        [SMEM] + [VMEM] * 4,
        [whole_updates],
        out_specs=[ANY],
        scratch=[pltpu.SemaphoreType.DMA((2,))],
        moved=2**19,
    )(plan_s(plan), up_d, up_l, over_d, mine)
    updates, new_momentum = run(
        finish_kernel,
        [SMEM] + [VMEM] * 8 + [ANY],
        [whole_updates, jax.ShapeDtypeStruct(momentum.shape, bf16)],
        out_specs=[ANY, ANY],
        scratch=[pltpu.SemaphoreType.DMA((3,))],
        moved=2**20,
        aliases={9: 0},
    )(plan_s(plan), faded, new, back, back_in, up_x, up_y, over_x, over_y, updates)
    return (updates, new_momentum)


def solution(mesh):
    placed = (P("dp", "expert", "fsdp", None), P("expert"), P(("dp", "expert", "fsdp"), None, None))
    n_replica, n_shard = mesh.shape["dp"], mesh.shape["fsdp"]

    def per_device(grads, owner_slot, momentum):
        mats, cap = grads.shape[1], momentum.shape[0]
        if (n_replica, n_shard, mats, cap) == (4, 2, 4, 1):
            return per_device_chips(grads, owner_slot, momentum)
        return per_device_general(grads, owner_slot, momentum)

    return jax.shard_map(
        per_device,
        mesh=mesh,
        in_specs=placed,
        out_specs=(P("expert", "fsdp", None), P(("dp", "expert", "fsdp"), None, None)),
        check_vma=False,
    )
```
